32 devices in a mesh: group: 2 (over x), tile: 16 (over z, y, core).
Axes of the slice: x: 2, y: 2, z: 4, core: 2. Of those that a mesh axis runs over, the one named last changes fastest.
Arguments:
- object_field: float32 [4, 2, 2048, 2048], P('group', None, 'tile'), parts along dimension 0, may hold values from -6 to 6
- probe: float32 [2, 256, 256], replicated, may hold values from -6 to 6
- measured: bfloat16 [64, 256, 256], P(('group', 'tile')), parts along dimension 0, may hold values from 0.099609375 to 3
- frame_table: int32 [64, 3], P(('group', 'tile')), parts along dimension 0, may hold values from 0 to 1792, as said below
- frame_count: int32 [32], P(('group', 'tile')), parts along dimension 0, may hold values from 0 to 2, as said below
Outputs:
- updated_object: float32 [4, 2, 2048, 2048], P('group', None, 'tile'), parts along dimension 0
- phase_map: float32 [4, 2048, 2048], P('group', 'tile'), parts along dimension 0
The draws below stay inside these ranges and needn't reach their ends.
There are 2 independent parts, one for each index of `group`. The reference program is written for one: setup_inputs(seed, part) draws one part's arguments, and reference() takes and returns one part's arrays. A program takes and returns all parts, laid end to end along the dimension named above; an argument that names none is the same for every part. Nothing has to cross between parts.
Inputs may be any that keep to these rules, and one draw needn't show every extreme that they name: `frame_table`: per slot: the row offset is below 128, and the frame's rows d * 128 + offset to that plus 256 - 1 and columns lie inside the projection; the angle is below 2. Only the first frame_count[d] slots of device d are live. `frame_count`: exactly 2 on some device in every draw; zero on every device d with d * 128 > 1792.
All inputs are finite; a program needn't handle non-finite values.
Results may differ from the reference program's by a relative error of at most 0.0009.
Values may be sent and summed in bfloat16 or wider, within the bound.
No kernel may reach another device: no remote copies, remote signals or barrier semaphores. Data moves between devices by JAX's collectives and lax.ppermute only.
A program may use at most 192 MiB of HBM per device.

```python
import math
import jax
import jax.numpy as jnp
from jax import lax

NP = 2048
FRAME = 256
ANGLES = 2
CAP = 2
SLOTS = 32
N_TILE = 16


def frame_layout(key):
    strip_rows = NP // N_TILE
    devices = jnp.arange(N_TILE, dtype=jnp.int32)
    spare_rows = jnp.clip(NP - FRAME - devices * strip_rows + 1, 0, strip_rows)
    subkeys = jax.random.split(jax.random.fold_in(key, 7), 6)
    first_draw = jax.random.randint(subkeys[0], (N_TILE,), 0, CAP, dtype=jnp.int32)
    second_draw = jax.random.randint(subkeys[1], (N_TILE,), 0, CAP, dtype=jnp.int32)
    counts = 1 + first_draw * second_draw // CAP
    busiest = jax.random.randint(subkeys[2], (), 0, N_TILE - FRAME // strip_rows + 1, dtype=jnp.int32)
    counts = jnp.where(devices == busiest, CAP, counts)
    counts = jnp.where(spare_rows > 0, counts, 0)
    offsets = jax.random.randint(subkeys[3], (N_TILE, CAP), 0, strip_rows, dtype=jnp.int32) % jnp.maximum(spare_rows, 1)[:, None]
    columns = jax.random.randint(subkeys[4], (N_TILE, CAP), 0, NP - FRAME + 1, dtype=jnp.int32)
    angle_ids = jax.random.randint(subkeys[5], (N_TILE, CAP), 0, ANGLES, dtype=jnp.int32)
    slot_table = jnp.stack([offsets, columns, angle_ids], -1).reshape(N_TILE * CAP, 3)
    return (slot_table.astype(jnp.int32), counts.astype(jnp.int32))


def draw_frame_table(key, part):
    return frame_layout(key)[0]


def draw_frame_count(key, part):
    return frame_layout(key)[1]


def block_levels(stream_key, dims, cuts, smallest, top_value):
    factor_of = 1.0
    for dim, parts in cuts:
        draws = jax.random.uniform(jax.random.fold_in(jax.random.fold_in(stream_key, 6), dim), (parts,), jnp.float32, smallest / len(cuts), top_value / len(cuts))
        factor_of = factor_of * jnp.repeat(jnp.exp(draws), dims[dim] // parts).reshape((-1,) + (1,) * (len(dims) - 1 - dim))
    return factor_of


def normal_values(own_key, shape, spread, most, pieces=(), kind=jnp.bfloat16):
    factor_of = block_levels(own_key, shape, pieces, -0.22, 0.18) if pieces else 1.0
    array = jax.random.normal(own_key, shape, jnp.float32) * spread * factor_of
    return jnp.minimum(jnp.maximum(array, -most), most).astype(kind)


def setup_inputs(seed: int = 0, part: int = 0) -> dict:
    arg_keys = jax.random.split(jax.random.key(seed), 6)
    part_splits = jax.random.split(jax.random.fold_in(arg_keys[5], part), 6)
    return {
        "object_field": normal_values(part_splits[0], (ANGLES, 2, NP, NP), 1.0, 6.0, ((2, 16),), jnp.float32),
        "probe": normal_values(arg_keys[1], (2, FRAME, FRAME), 1.0, 6.0, (), jnp.float32),
        "measured": jnp.clip(jnp.exp(math.log(3.0) - 3.4051113 * jax.random.uniform(part_splits[2], (SLOTS, FRAME, FRAME), jnp.float32) ** block_levels(part_splits[2], (SLOTS, FRAME, FRAME), ((0, 16),), -0.2, 0.2)), 0.099609375, 3.0).astype(jnp.bfloat16),
        "frame_table": draw_frame_table(jax.random.fold_in(jax.random.fold_in(arg_keys[5], part), 71), part),
        "frame_count": draw_frame_count(jax.random.fold_in(jax.random.fold_in(arg_keys[5], part), 71), part),
    }


magnitude_floor = 0.5
soften_term = 0.5
screen_term = 0.0001
epsilon_term = 1e-06

def fourier_tables(frame_side):
    indices = jnp.arange(frame_side, dtype=jnp.int32)
    products = indices[:, None] * indices[None, :] % frame_side
    phases = products.astype(jnp.float32) * (-2.0 * math.pi / frame_side)
    norm_scale = 1.0 / math.sqrt(frame_side)
    return ((jnp.cos(phases) * norm_scale).astype(jnp.bfloat16), (jnp.sin(phases) * norm_scale).astype(jnp.bfloat16))

def complex_left(table_re, table_im, operand):
    side = table_re.shape[0]
    stacked = jnp.concatenate([table_re, table_im], 0)
    joined = jnp.concatenate([operand[0], operand[1]], 1)
    products = jnp.dot(stacked, joined, preferred_element_type=jnp.float32)
    return jnp.stack([products[:side, :side] - products[side:, side:], products[:side, side:] + products[side:, :side]])

def complex_right(operand, table_re, table_im):
    side = table_re.shape[0]
    stacked = jnp.concatenate([operand[0], operand[1]], 0)
    joined = jnp.concatenate([table_re, table_im], 1)
    products = jnp.dot(stacked, joined, preferred_element_type=jnp.float32)
    return jnp.stack([products[:side, :side] - products[side:, side:], products[:side, side:] + products[side:, :side]])

def correct_frame(exit_field, magnitude, fourier):
    cos_part, sin_part = fourier
    half_spectrum = complex_left(cos_part, sin_part, exit_field).astype(jnp.bfloat16)
    spectrum = complex_right(half_spectrum, cos_part, sin_part)
    amplitude = jnp.sqrt(spectrum[0] * spectrum[0] + spectrum[1] * spectrum[1])
    factor = magnitude.astype(spectrum.dtype) / jnp.maximum(amplitude, magnitude_floor) - 1.0
    change = (spectrum * factor[None]).astype(jnp.bfloat16)
    half_back = complex_left(cos_part, -sin_part, change).astype(jnp.bfloat16)
    return complex_right(half_back, cos_part, -sin_part)

def exit_wave(probe, patch):
    object_part = patch.astype(probe.dtype)
    real_part = probe[0] * object_part[0] - probe[1] * object_part[1]
    imag_part = probe[0] * object_part[1] + probe[1] * object_part[0]
    return jnp.stack([real_part, imag_part]).astype(jnp.bfloat16)

def object_step(probe, correction, probe_peak):
    real_part = (probe[0] * correction[0] + probe[1] * correction[1]) / probe_peak
    imag_part = (probe[0] * correction[1] - probe[1] * correction[0]) / probe_peak
    return jnp.stack([real_part, imag_part])

def phase_bond(first_cell, second_cell):
    cross_term = first_cell[:, 0] * second_cell[:, 1] - first_cell[:, 1] * second_cell[:, 0]
    power_sum = first_cell[:, 0] ** 2 + first_cell[:, 1] ** 2 + second_cell[:, 0] ** 2 + second_cell[:, 1] ** 2 + soften_term
    return 2.0 * cross_term / power_sum

def cosine_last(values):
    length = values.shape[-1]
    mirrored = jnp.concatenate([values, jnp.flip(values, -1)], -1)
    spectrum = jnp.fft.fft(mirrored, axis=-1)[..., :length]
    freqs = jnp.arange(length, dtype=jnp.int32).astype(values.dtype)
    twisted = jnp.real(spectrum * jnp.exp(-1j * math.pi * freqs / (2 * length)))
    norm_scale = jnp.where(freqs == 0, math.sqrt(1.0 / length), math.sqrt(2.0 / length)) * 0.5
    return (twisted * norm_scale).astype(values.dtype)

def inverse_last(coeffs):
    length = coeffs.shape[-1]
    freqs = jnp.arange(length, dtype=jnp.int32).astype(coeffs.dtype)
    norm_scale = jnp.where(freqs == 0, math.sqrt(1.0 / length), math.sqrt(2.0 / length))
    weighted = coeffs * norm_scale * jnp.exp(1j * math.pi * freqs / (2 * length))
    padded = jnp.concatenate([weighted, jnp.zeros_like(weighted)], -1)
    values = jnp.real(jnp.fft.ifft(padded, axis=-1)[..., :length]) * (2 * length)
    return values.astype(coeffs.dtype)

def reference(object_field, probe, measured, frame_table, frame_count):
    window_object = object_field.astype(jnp.bfloat16)
    fourier = fourier_tables(FRAME)
    probe_peak = jnp.max(probe[0] * probe[0] + probe[1] * probe[1]) + epsilon_term
    strip_rows = NP // N_TILE
    anchor = jnp.zeros((), jnp.int32)

    def visit(slot_index, deposits):
        slot_index = jnp.asarray(slot_index).astype(jnp.int32)
        owner = slot_index // CAP
        live = slot_index % CAP < frame_count[owner]

        def apply(current_sum):
            record = frame_table[slot_index]
            corner = (record[2].astype(jnp.int32), anchor, (owner * strip_rows + record[0]).astype(jnp.int32), record[1].astype(jnp.int32))
            patch = lax.dynamic_slice(window_object, corner, (1, 2, FRAME, FRAME))[0]
            correction = correct_frame(exit_wave(probe, patch), measured[slot_index], fourier)
            update = object_step(probe, correction, probe_peak)
            current = lax.dynamic_slice(current_sum, corner, (1, 2, FRAME, FRAME))
            return lax.dynamic_update_slice(current_sum, current + update[None], corner)
        return lax.cond(live, apply, lambda current_sum: current_sum, deposits)
    deposits = lax.fori_loop(0, SLOTS, visit, jnp.zeros(object_field.shape, object_field.dtype))
    updated_object = object_field + deposits
    padded = jnp.pad(updated_object, ((0, 0), (0, 0), (1, 1), (1, 1)))
    row_grad = phase_bond(padded[:, :, :-1, 1:-1], padded[:, :, 1:, 1:-1])
    col_grad = phase_bond(padded[:, :, 1:-1, :-1], padded[:, :, 1:-1, 1:])
    source = -(row_grad[:, 1:] - row_grad[:, :-1] + col_grad[:, :, 1:] - col_grad[:, :, :-1])
    along_rows = jnp.swapaxes(cosine_last(jnp.swapaxes(source, 1, 2)), 1, 2)
    both_dims = cosine_last(along_rows)
    freqs = jnp.arange(NP, dtype=jnp.int32).astype(source.dtype)
    eigen = 2.0 - 2.0 * jnp.cos(freqs * (math.pi / NP))
    coefficients = both_dims / (screen_term + eigen[None, :, None] + eigen[None, None, :])
    back_rows = jnp.swapaxes(inverse_last(jnp.swapaxes(coefficients, 1, 2)), 1, 2)
    phase_map = inverse_last(back_rows)
    return (updated_object, phase_map)
```

```python
import functools
import math

import jax
import jax.numpy as jnp
import ml_dtypes
import numpy as np
from jax import lax
from jax.experimental import pallas as pl
from jax.experimental.pallas import tpu as pltpu
from jax.sharding import PartitionSpec as P

magnitude_floor = 0.5
soften_term = 0.5
screen_term = 0.0001
epsilon_term = 1e-06
LANES = 128
SEG = 8
PAD = 8
f32 = jnp.float32
bf16 = jnp.bfloat16
VMEM_SPEC = pl.BlockSpec(memory_space=pltpu.VMEM)
SMEM_SPEC = pl.BlockSpec(memory_space=pltpu.SMEM)
ANY_SPEC = pl.BlockSpec(memory_space=pl.ANY)
PARAMS = pltpu.CompilerParams(vmem_limit_bytes=52 * 1024 * 1024)


def split_table(table):
    high = table.astype(ml_dtypes.bfloat16)
    low = (table - high.astype(np.float64)).astype(ml_dtypes.bfloat16)
    return np.stack([high, low])


def fourier_blocks(side):
    index = np.arange(side)
    phase = (index[:, None] * index[None, :] % side) * (-2.0 * math.pi / side)
    cos_part = np.cos(phase) / math.sqrt(side)
    sin_part = np.sin(phase) / math.sqrt(side)
    left = np.block([[cos_part, -sin_part], [sin_part, cos_part]])
    right = np.block([[cos_part, sin_part], [-sin_part, cos_part]])
    return left.astype(ml_dtypes.bfloat16), right.astype(ml_dtypes.bfloat16)


def cosine_halves(grid):
    half = grid // 2
    freqs = np.arange(grid)
    pixels = np.arange(half)
    phase = (2 * pixels[None, :] + 1) * freqs[:, None] % (4 * grid)
    scale = np.where(freqs == 0, math.sqrt(1.0 / grid), math.sqrt(2.0 / grid))
    table = scale[:, None] * np.cos(phase * (math.pi / (2 * grid)))
    return np.stack([table[0::2], table[1::2]])


def decay_tables(grid, strip):
    freqs = np.concatenate([np.arange(0, grid, 2), np.arange(1, grid, 2)])
    mu = screen_term + 4.0 * np.sin(freqs * (math.pi / (2 * grid))) ** 2
    root = 1.0 + mu / 2 - np.sqrt(mu + mu * mu / 4)
    log_root = np.log(root)
    steps = strip // SEG
    devices = grid // strip

    def power(exponents):
        return np.exp(np.maximum(log_root[None, :] * np.asarray(exponents)[:, None], -80.0)) * (
            log_root[None, :] * np.asarray(exponents)[:, None] > -80.0
        )

    scan = np.concatenate([power([1, steps, 2 * steps, 4 * steps]), (root / (1 - root * root))[None]])
    inner = power(np.arange(1, steps + 1))
    segs = power(steps * np.arange(SEG))
    strips = power(strip * np.arange(devices + 1))
    closing = 1.0 / (1.0 - power([2 * grid]))
    as32 = lambda x: x.astype(np.float32)
    return as32(scan), as32(inner), as32(segs), as32(segs[::-1]), as32(strips), as32(closing)


def clip(value, top):
    return jnp.minimum(jnp.maximum(value, 0), top)


def extract_kernel(tab, field, out, raw, sems):
    caps, _, strip, frame = out.shape
    angles, grid = field.shape[0], field.shape[3]
    wide = frame + LANES
    copies = []
    shifts = []
    for slot in range(caps):
        column = clip(tab[3 * slot + 1], grid - frame)
        angle = clip(tab[3 * slot + 2], angles - 1)
        block = jnp.minimum(column // LANES, (grid - wide) // LANES)
        shifts.append(column - block * LANES)
        start = pl.multiple_of(block * LANES, LANES)
        copies.append(
            pltpu.make_async_copy(
                field.at[angle, :, :, pl.ds(start, wide)], raw.at[slot], sems.at[slot]
            )
        )
    for copy in copies:
        copy.start()
    for slot in range(caps):
        copies[slot].wait()
        for part in range(2):
            moved = pltpu.roll(raw[slot, part], lax.rem(wide - shifts[slot], wide), axis=1)
            out[slot, part] = moved[:, :frame].astype(bf16)


def extract(tab, field, caps, frame):
    angles, _, strip, grid = field.shape
    return pl.pallas_call(
        extract_kernel,
        out_shape=jax.ShapeDtypeStruct((caps, 2, strip, frame), bf16),
        in_specs=[SMEM_SPEC, ANY_SPEC],
        out_specs=VMEM_SPEC,
        scratch_shapes=[
            pltpu.VMEM((caps, 2, strip, frame + LANES), f32),
            pltpu.SemaphoreType.DMA((caps,)),
        ],
        compiler_params=PARAMS,
        name="extract",
    )(tab, field)


def frame_kernel(reach, center, tab, probe, measured, left, right, *rest):
    windows = rest[: reach + 1]
    first_piece = rest[reach + 1]
    pieces = rest[reach + 2 : 2 * reach + 3]
    window_buf, update_buf = rest[2 * reach + 3 :]
    caps, frame = measured.shape[0], measured.shape[1]
    strip = windows[0].shape[2]
    blocks = frame // LANES
    count = tab[3 * caps]
    probe_re, probe_im = probe[0], probe[1]
    peak = jnp.max(probe_re * probe_re + probe_im * probe_im) + epsilon_term
    for slot in range(caps):
        update_buf[...] = jnp.zeros_like(update_buf)

        @pl.when(slot < count)
        def _():
            offset = clip(tab[3 * slot], strip - 1)
            for j in range(reach + 1):
                for part in range(2):
                    for k in range(blocks):
                        window_buf[part, k, j * strip : (j + 1) * strip] = windows[j][
                            slot, part, :, k * LANES : (k + 1) * LANES
                        ].astype(f32)
            obj_re, obj_im = (
                jnp.concatenate(
                    [window_buf[part, k, pl.ds(offset, frame), :] for k in range(blocks)], axis=1
                )
                for part in range(2)
            )
            wave = jnp.concatenate(
                [
                    (probe_re * obj_re - probe_im * obj_im).astype(bf16),
                    (probe_re * obj_im + probe_im * obj_re).astype(bf16),
                ],
                axis=0,
            )

            def both(first, second, rows):
                first_half = jnp.dot(first, rows, preferred_element_type=f32).astype(bf16)
                beside = jnp.concatenate([first_half[:frame], first_half[frame:]], axis=1)
                return jnp.dot(beside, second, preferred_element_type=f32)

            spectrum = both(left[...], right[...], wave)
            spec_re, spec_im = spectrum[:, :frame], spectrum[:, frame:]
            power = spec_re * spec_re + spec_im * spec_im
            factor = (
                measured[slot].astype(f32) * lax.rsqrt(jnp.maximum(power, magnitude_floor**2)) - 1.0
            )
            change = jnp.concatenate(
                [(spec_re * factor).astype(bf16), (spec_im * factor).astype(bf16)], axis=0
            )
            correction = both(right[...], left[...], change)
            corr_re, corr_im = correction[:, :frame], correction[:, frame:]
            update = (
                (probe_re * corr_re + probe_im * corr_im) / peak,
                (probe_re * corr_im - probe_im * corr_re) / peak,
            )
            for part in range(2):
                for k in range(blocks):
                    update_buf[part, k, pl.ds(2 * PAD + offset, frame), :] = update[part][
                        :, k * LANES : (k + 1) * LANES
                    ]

        for part in range(2):
            for k in range(blocks):
                lanes = slice(k * LANES, (k + 1) * LANES)
                first_piece[slot, part, :, lanes] = update_buf[part, k, 2 * PAD : 4 * PAD].astype(
                    first_piece.dtype
                )
                for j in range(reach + 1):
                    pieces[j][slot, part, :, lanes] = update_buf[
                        part, k, j * strip + PAD : (j + 1) * strip + 3 * PAD
                    ].astype(pieces[j].dtype)


def run_frames(tab, probe, measured, windows, center):
    reach = len(windows) - 1
    caps, frame = measured.shape[0], measured.shape[1]
    strip = windows[0].shape[2]
    left, right = fourier_blocks(frame)
    rows = (reach + 1) * strip
    piece = lambda j: jax.ShapeDtypeStruct(
        (caps, 2, strip + 2 * PAD, frame), f32 if j == center else bf16
    )
    return pl.pallas_call(
        functools.partial(frame_kernel, reach, center),
        out_shape=[jax.ShapeDtypeStruct((caps, 2, 2 * PAD, frame), bf16)]
        + [piece(j) for j in range(reach + 1)],
        in_specs=[SMEM_SPEC] + [VMEM_SPEC] * (5 + reach),
        out_specs=[VMEM_SPEC] * (reach + 2),
        scratch_shapes=[
            pltpu.VMEM((2, frame // LANES, rows, LANES), f32),
            pltpu.VMEM((2, frame // LANES, rows + 4 * PAD, LANES), f32),
        ],
        compiler_params=PARAMS,
        name="frames",
    )(tab, probe, measured, jnp.asarray(left), jnp.asarray(right), *windows)


def reversed_lanes(values):
    index = LANES - 1 - lax.broadcasted_iota(jnp.int32, values.shape, 1)
    return jnp.take_along_axis(values, index, axis=1)


def split_pair(values):
    high = values.astype(bf16)
    return high, (values - high.astype(f32)).astype(bf16)


def three_pass(rows, count, high, low):
    both = jnp.dot(rows, high, preferred_element_type=f32)
    return both[:count] + both[count:] + jnp.dot(rows[:count], low, preferred_element_type=f32)


def update_kernel(reach, tabs, field, top, bottom, scan, table_hbm, *rest):
    first_piece = rest[0]
    pieces = rest[1 : reach + 2]
    updated, inner, carry_y, carry_z, ends = rest[reach + 2 : reach + 7]
    ext, row_bond, source, rows_in, table, load_sems, store_sems, table_sems = rest[reach + 7 :]
    angles, _, strip, grid = field.shape
    blocks = grid // LANES
    half_blocks = blocks // 2
    half = grid // 2
    steps = strip // SEG
    count = angles * strip
    caps = pieces[0].shape[0]
    frame = pieces[0].shape[3]
    frame_blocks = frame // LANES

    def load(a, b):
        start = b * LANES
        return pltpu.make_async_copy(
            field.at[a, :, :, pl.ds(start, LANES)],
            ext.at[a, :, b, pl.ds(PAD, strip), :],
            load_sems.at[a, b],
        )

    def store(a, b):
        start = b * LANES
        return pltpu.make_async_copy(
            ext.at[a, :, b, pl.ds(PAD, strip), :],
            updated.at[a, :, :, pl.ds(start, LANES)],
            store_sems.at[a, b],
        )

    def load_table(h, k):
        return pltpu.make_async_copy(table_hbm.at[k, h], table.at[k, h], table_sems.at[k, h])

    for a in range(angles):
        for b in range(blocks):
            load(a, b).start()
    for h in range(2):
        for k in range(2):
            load_table(h, k).start()

    for a in range(angles):
        for part in range(2):
            for b in range(blocks):
                lanes = slice(b * LANES, (b + 1) * LANES)
                ext[a, part, b, PAD - 1 : PAD, :] = top[a, part, :, lanes]
                ext[a, part, b, PAD + strip : PAD + strip + 1, :] = bottom[a, part, :, lanes]
            ext[a, part, blocks] = jnp.zeros((strip + 2 * PAD, LANES), f32)
    for a in range(angles):
        for b in range(blocks):
            load(a, b).wait()

    def add_piece(piece, tab_row, slot, first_row, rows):
        @pl.when(slot < tabs[tab_row, 3 * caps])
        def _():
            column = clip(tabs[tab_row, 3 * slot + 1], grid - frame)
            angle = clip(tabs[tab_row, 3 * slot + 2], angles - 1)
            block = jnp.minimum(column // LANES, blocks - frame_blocks - 1)
            shift = column - block * LANES
            for part in range(2):
                values = piece[slot, part, :rows].astype(f32)
                values = jnp.concatenate([values, jnp.zeros((rows, LANES), f32)], axis=1)
                values = pltpu.roll(values, shift, axis=1)
                for k in range(frame_blocks + 1):
                    spot = ext.at[angle, part, block + k, first_row : first_row + rows]
                    spot[...] += values[:, k * LANES : (k + 1) * LANES]

    for slot in range(caps):
        add_piece(first_piece, 0, slot, PAD + strip, PAD)
        for j in range(reach + 1):
            add_piece(pieces[j], j + 1, slot, 0, strip + 2 * PAD)

    for a in range(angles):
        for b in range(blocks):
            store(a, b).start()

    lane = lax.broadcasted_iota(jnp.int32, (strip, LANES), 1)

    def bond(re, im, power, re_to, im_to, power_to):
        whole = power + power_to
        guess = pl.reciprocal(whole, approx=True)
        guess = guess * (2.0 - whole * guess)
        return (re * im_to - im * re_to) * guess

    def reach_right(now, after):
        return pltpu.roll(jnp.where(lane == 0, after, now), LANES - 1, axis=1)

    for a in range(angles):

        def columns(b, before, a=a):
            tall = strip + PAD
            re, im = ext[a, 0, b, 0:tall], ext[a, 1, b, 0:tall]
            re_to, im_to = ext[a, 0, b, 1 : tall + 1], ext[a, 1, b, 1 : tall + 1]
            power = 0.5 * (re * re + im * im) + 0.25 * soften_term
            power_to = 0.5 * (re_to * re_to + im_to * im_to) + 0.25 * soften_term
            row_bond[0:tall] = bond(re, im, power, re_to, im_to, power_to)
            re, im, power = re[PAD:], im[PAD:], power[PAD:]
            re_to = reach_right(re, ext[a, 0, b + 1, PAD:tall])
            im_to = reach_right(im, ext[a, 1, b + 1, PAD:tall])
            power_to = 0.5 * (re_to * re_to + im_to * im_to) + 0.25 * soften_term
            here = bond(re, im, power, re_to, im_to, power_to)
            shifted = pltpu.roll(jnp.where(lane == LANES - 1, before, here), 1, axis=1)
            source[a, b] = (
                row_bond[PAD - 1 : tall - 1] - row_bond[PAD:tall] + shifted - here
            )
            return here

        lax.fori_loop(0, blocks, columns, jnp.zeros((strip, LANES), f32))

    def fold(b, _):
        lanes = pl.ds(pl.multiple_of(b * LANES, LANES), LANES)
        for a in range(angles):
            for t in range(0, steps, 2):
                lower = jnp.concatenate(
                    [source[a, b, pl.ds(t + i, SEG, stride=steps), :] for i in range(2)], 0
                )
                upper = jnp.concatenate(
                    [
                        source[a, blocks - 1 - b, pl.ds(t + i, SEG, stride=steps), :]
                        for i in range(2)
                    ],
                    0,
                )
                upper = reversed_lanes(upper)
                at = a * strip + t * SEG
                for h, values in enumerate((lower + upper, lower - upper)):
                    high, low = split_pair(values)
                    rows_in[h, at : at + 2 * SEG, lanes] = high
                    rows_in[h, count + at : count + at + 2 * SEG, lanes] = low
        return 0

    lax.fori_loop(0, half_blocks, fold, 0)

    wide = min(2 * LANES, half)
    sub = lax.broadcasted_iota(jnp.int32, (SEG, wide), 0)
    for h in range(2):
        for k in range(2):
            load_table(h, k).wait()

        def transform(c, _, h=h):
            lanes = pl.ds(pl.multiple_of(c * wide, wide), wide)
            spots = pl.ds(pl.multiple_of(h * half + c * wide, wide), wide)
            values = three_pass(rows_in[h], count, table[0, h, :, lanes], table[1, h, :, lanes])
            root = jnp.broadcast_to(scan[0:1, spots], (SEG, wide))
            for a in range(angles):
                terms = [
                    values[a * strip + t * SEG : a * strip + (t + 1) * SEG] for t in range(steps)
                ]
                down = [terms[0]]
                for t in range(1, steps):
                    down.append(terms[t] + root * down[-1])
                up = terms[steps - 1]
                inner[a, (steps - 1) * SEG : steps * SEG, spots] = down[steps - 1]
                for t in range(steps - 2, -1, -1):
                    after = root * up
                    inner[a, t * SEG : (t + 1) * SEG, spots] = down[t] + after
                    up = terms[t] + after
                tail_y, tail_z = down[steps - 1], up
                for i, k in enumerate((1, 2, 4)):
                    factor = scan[i + 1 : i + 2, spots]
                    tail_y = tail_y + jnp.where(
                        sub >= k, factor * pltpu.roll(tail_y, k, axis=0), 0.0
                    )
                    tail_z = tail_z + jnp.where(
                        sub < SEG - k, factor * pltpu.roll(tail_z, SEG - k, axis=0), 0.0
                    )
                carry_y[a, :, spots] = jnp.where(sub >= 1, pltpu.roll(tail_y, 1, axis=0), 0.0)
                carry_z[a, :, spots] = jnp.where(
                    sub < SEG - 1, pltpu.roll(tail_z, SEG - 1, axis=0), 0.0
                )
                ends[0, a : a + 1, spots] = tail_z[0:1]
                ends[1, a : a + 1, spots] = tail_y[SEG - 1 : SEG]
            return 0

        lax.fori_loop(0, half // wide, transform, 0)

    for a in range(angles):
        for b in range(blocks):
            store(a, b).wait()


def run_update(tabs, field, top, bottom, scan, table, first_piece, pieces):
    angles, _, strip, grid = field.shape
    reach = len(pieces) - 1
    blocks = grid // LANES
    half = grid // 2
    return pl.pallas_call(
        functools.partial(update_kernel, reach),
        out_shape=[
            jax.ShapeDtypeStruct(field.shape, f32),
            jax.ShapeDtypeStruct((angles, strip, grid), f32),
            jax.ShapeDtypeStruct((angles, SEG, grid), f32),
            jax.ShapeDtypeStruct((angles, SEG, grid), f32),
            jax.ShapeDtypeStruct((2, angles, grid), f32),
        ],
        in_specs=[SMEM_SPEC, ANY_SPEC, VMEM_SPEC, VMEM_SPEC, VMEM_SPEC, ANY_SPEC]
        + [VMEM_SPEC] * (reach + 2),
        out_specs=[ANY_SPEC] + [VMEM_SPEC] * 4,
        scratch_shapes=[
            pltpu.VMEM((angles, 2, blocks + 1, strip + 2 * PAD, LANES), f32),
            pltpu.VMEM((strip + 2 * PAD, LANES), f32),
            pltpu.VMEM((angles, blocks, strip, LANES), f32),
            pltpu.VMEM((2, 2 * angles * strip, half), bf16),
            pltpu.VMEM((2, 2, half, half), bf16),
            pltpu.SemaphoreType.DMA((angles, blocks)),
            pltpu.SemaphoreType.DMA((angles, blocks)),
            pltpu.SemaphoreType.DMA((2, 2)),
        ],
        compiler_params=PARAMS,
        name="update",
    )(tabs, field, top, bottom, scan, table, first_piece, *pieces)


def phase_kernel(inner, carry_y, carry_z, enter, scan, powers, segs, segs_back, table_hbm, out, rest, rows_in, table, sems):
    angles, strip, grid = inner.shape
    half = grid // 2
    steps = strip // SEG
    count = angles * strip
    half_blocks = half // LANES

    def load_table(h, k):
        return pltpu.make_async_copy(table_hbm.at[k, h], table.at[k, h], sems.at[k, h])

    for h in range(2):
        for k in range(2):
            load_table(h, k).start()

    def solve(b, _):
        spots = pl.ds(pl.multiple_of(b * LANES, LANES), LANES)
        scale = scan[4:5, spots]
        for a in range(angles):
            from_y = scale * (carry_y[a, :, spots] + segs[:, spots] * enter[0, a : a + 1, spots])
            from_z = scale * (carry_z[a, :, spots] + segs_back[:, spots] * enter[1, a : a + 1, spots])
            for t in range(steps):
                rest[a, b, pl.ds(t, SEG, stride=steps), :] = (
                    scale * inner[a, t * SEG : (t + 1) * SEG, spots]
                    + powers[t : t + 1, spots] * from_y
                    + powers[steps - 1 - t : steps - t, spots] * from_z
                )
        return 0

    lax.fori_loop(0, 2 * half_blocks, solve, 0)

    def split(b, _):
        lanes = pl.ds(pl.multiple_of(b * LANES, LANES), LANES)
        for h in range(2):
            for a in range(angles):
                high, low = split_pair(rest[a, h * half_blocks + b])
                rows_in[h, a * strip : (a + 1) * strip, lanes] = high
                rows_in[h, count + a * strip : count + (a + 1) * strip, lanes] = low
        return 0

    lax.fori_loop(0, half_blocks, split, 0)
    for h in range(2):
        for k in range(2):
            load_table(h, k).wait()
    wide = min(2 * LANES, half)

    def back(c, _):
        lanes = pl.ds(pl.multiple_of(c * wide, wide), wide)
        even, odd = (
            three_pass(rows_in[h], count, table[0, h, :, lanes], table[1, h, :, lanes])
            for h in range(2)
        )
        mirrored = even - odd
        plain = even + odd
        for a in range(angles):
            out[a, :, lanes] = plain[a * strip : (a + 1) * strip]
            for k in range(wide // LANES):
                spot = pl.ds(
                    pl.multiple_of(grid - (k + 1) * LANES - c * wide, LANES), LANES
                )
                out[a, :, spot] = reversed_lanes(
                    mirrored[a * strip : (a + 1) * strip, k * LANES : (k + 1) * LANES]
                )
        return 0

    lax.fori_loop(0, half // wide, back, 0)


def run_phase(inner, carry_y, carry_z, enter, scan, powers, segs, segs_back, table):
    angles, strip, grid = inner.shape
    half = grid // 2
    return pl.pallas_call(
        phase_kernel,
        out_shape=jax.ShapeDtypeStruct((angles, strip, grid), f32),
        in_specs=[VMEM_SPEC] * 8 + [ANY_SPEC],
        out_specs=VMEM_SPEC,
        scratch_shapes=[
            pltpu.VMEM((angles, grid // LANES, strip, LANES), f32),
            pltpu.VMEM((2, 2 * angles * strip, half), bf16),
            pltpu.VMEM((2, 2, half, half), bf16),
            pltpu.SemaphoreType.DMA((2, 2)),
        ],
        compiler_params=PARAMS,
        name="phase",
    )(inner, carry_y, carry_z, enter, scan, powers, segs, segs_back, table)


def passed_along(x, by):
    size = lax.axis_size("tile")
    pairs = [(i, i + by) for i in range(size) if 0 <= i + by < size]
    return lax.ppermute(x, "tile", pairs)


def entering_values(ends, strips, closing):
    size = lax.axis_size("tile")
    me = lax.axis_index("tile")
    head, tail = ends[0], ends[1]
    enter_y = jnp.zeros_like(head)
    enter_z = jnp.zeros_like(head)
    row = lambda i: lax.dynamic_slice_in_dim(strips, i, 1, 0)
    width = 1
    while width < size:
        other = lax.ppermute(
            jnp.stack([head, tail]), "tile", [(i, i ^ width) for i in range(size)]
        )
        head_to, tail_to = other[0], other[1]
        second = (me & width) != 0
        before = me & (width - 1)
        span = strips[width : width + 1]
        enter_y = enter_y + jnp.where(second, row(before) * tail_to, 0.0)
        enter_z = enter_z + jnp.where(second, 0.0, row(width - 1 - before) * head_to)
        head, tail = (
            jnp.where(second, head_to + span * head, head + span * head_to),
            jnp.where(second, tail + span * tail_to, tail_to + span * tail),
        )
        width *= 2
    whole = strips[size : size + 1]
    enter_y = enter_y + row(me) * (head + whole * tail) * closing
    enter_z = enter_z + row(size - 1 - me) * (tail + whole * head) * closing
    return jnp.stack([enter_y, enter_z])


def body(object_field, probe, measured, frame_table, frame_count):
    angles, _, strip, grid = object_field.shape
    caps, frame = measured.shape[0], measured.shape[1]
    reach = frame // strip
    center = reach // 2
    table = cosine_halves(grid)
    forward_table = jnp.asarray(split_table(np.swapaxes(table, 1, 2)))
    back_table = jnp.asarray(split_table(table))
    scan, powers, segs, segs_back, strips, closing = (
        jnp.asarray(x) for x in decay_tables(grid, strip)
    )

    own_tab = jnp.concatenate([frame_table.reshape(-1), frame_count])
    tabs = {j: own_tab if j == 0 else passed_along(own_tab, j) for j in range(-1, reach + 1)}
    measured_here = passed_along(measured, center)
    bottom = passed_along(object_field[:, :, :1], -1)
    top = passed_along(object_field[:, :, strip - 1 :], 1)
    windows = []
    for j in range(reach + 1):
        window = extract(tabs[j], object_field, caps, frame)
        windows.append(window if j == center else passed_along(window, center - j))
    first_piece, *pieces = run_frames(tabs[center], probe, measured_here, windows, center)
    first_piece = passed_along(first_piece, -1 - center)
    pieces = [
        piece if j == center else passed_along(piece, j - center) for j, piece in enumerate(pieces)
    ]
    all_tabs = jnp.stack([tabs[j] for j in range(-1, reach + 1)])
    updated, inner, carry_y, carry_z, ends = run_update(
        all_tabs, object_field, top, bottom, scan, forward_table, first_piece, pieces
    )
    enter = entering_values(ends, strips, closing)
    phase_map = run_phase(
        inner, carry_y, carry_z, enter, scan, powers, segs, segs_back, back_table
    )
    return (updated, phase_map)


def solution(mesh):
    return jax.shard_map(
        body,
        mesh=mesh,
        in_specs=(
            P("group", None, "tile", None),
            P(),
            P(("group", "tile"), None, None),
            P(("group", "tile"), None),
            P(("group", "tile")),
        ),
        out_specs=(P("group", None, "tile", None), P("group", "tile", None)),
        check_vma=False,
    )
```

```python
import functools
import math

import jax
import jax.numpy as jnp
import ml_dtypes
import numpy as np
from jax import lax
from jax.experimental import pallas as pl
from jax.experimental.pallas import tpu as pltpu
from jax.sharding import PartitionSpec as P

magnitude_floor = 0.5
soften_term = 0.5
screen_term = 0.0001
epsilon_term = 1e-06
LANES = 128
SEG = 8
PAD = 8
f32 = jnp.float32
bf16 = jnp.bfloat16
VMEM_SPEC = pl.BlockSpec(memory_space=pltpu.VMEM)
SMEM_SPEC = pl.BlockSpec(memory_space=pltpu.SMEM)
ANY_SPEC = pl.BlockSpec(memory_space=pl.ANY)
PARAMS = pltpu.CompilerParams(vmem_limit_bytes=26 * 1024 * 1024)
UPDATE_PARAMS = pltpu.CompilerParams(vmem_limit_bytes=44 * 1024 * 1024)
PHASE_PARAMS = pltpu.CompilerParams(vmem_limit_bytes=46 * 1024 * 1024)
DIGIT = 64
CODE_ROWS = 16
FIELDS = 4
BATCH = 8


def cost(micros):
    return pl.CostEstimate(flops=0, bytes_accessed=int(micros * 3.0e6), transcendentals=0)


def split_table(table):
    high = table.astype(ml_dtypes.bfloat16)
    low = (table - high.astype(np.float64)).astype(ml_dtypes.bfloat16)
    return np.stack([high, low])


def fourier_blocks(side):
    index = np.arange(side)
    phase = (index[:, None] * index[None, :] % side) * (-2.0 * math.pi / side)
    cos_part = np.cos(phase) / math.sqrt(side)
    sin_part = np.sin(phase) / math.sqrt(side)
    left = np.block([[cos_part, -sin_part], [sin_part, cos_part]])
    right = np.block([[cos_part, sin_part], [-sin_part, cos_part]])
    return left.astype(ml_dtypes.bfloat16), right.astype(ml_dtypes.bfloat16)


def cosine_halves(grid):
    half = grid // 2
    freqs = np.arange(grid)
    pixels = np.arange(half)
    phase = (2 * pixels[None, :] + 1) * freqs[:, None] % (4 * grid)
    scale = np.where(freqs == 0, math.sqrt(1.0 / grid), math.sqrt(2.0 / grid))
    table = scale[:, None] * np.cos(phase * (math.pi / (2 * grid)))
    return np.stack([table[0::2], table[1::2]])


def decay_tables(grid, strip):
    freqs = np.concatenate([np.arange(0, grid, 2), np.arange(1, grid, 2)])
    mu = screen_term + 4.0 * np.sin(freqs * (math.pi / (2 * grid))) ** 2
    root = 1.0 + mu / 2 - np.sqrt(mu + mu * mu / 4)
    log_root = np.log(root)
    steps = strip // SEG
    devices = grid // strip

    def power(exponents):
        return np.exp(np.maximum(log_root[None, :] * np.asarray(exponents)[:, None], -80.0)) * (
            log_root[None, :] * np.asarray(exponents)[:, None] > -80.0
        )

    scan = np.concatenate(
        [
            power([1, steps, 2 * steps, 4 * steps]),
            (2 * root / (1 - root * root))[None],
            (1 / root)[None],
            power([strip]),
        ]
    )
    inner = power(np.arange(1, steps + 1))
    segs = power(steps * np.arange(SEG))
    strips = power(strip * np.arange(devices + 1))
    closing = 1.0 / (1.0 - power([2 * grid]))
    as32 = lambda x: x.astype(np.float32)
    return as32(scan), as32(inner), as32(segs), as32(segs[::-1]), as32(strips), as32(closing)


def clip(value, top):
    return jnp.minimum(jnp.maximum(value, 0), top)


def window_copies(tab, field, raw, sems):
    caps, wide = raw.shape[0], raw.shape[3]
    frame = wide - LANES
    angles, grid = field.shape[0], field.shape[3]
    copies = []
    for slot in range(caps):
        column = clip(tab(slot, 1), grid - frame)
        angle = clip(tab(slot, 2), angles - 1)
        block = jnp.minimum(column // LANES, (grid - wide) // LANES)
        start = pl.multiple_of(block * LANES, LANES)
        copy = pltpu.make_async_copy(
            field.at[angle, :, :, pl.ds(start, wide)], raw.at[slot], sems.at[slot]
        )
        copy.start()
        copies.append((copy, lax.rem(wide - (column - block * LANES), wide)))
    return copies


def window_values(copies, raw, slot, part):
    wide = raw.shape[3]
    return pltpu.roll(raw[slot, part], copies[slot][1], axis=1)[:, : wide - LANES].astype(bf16)


def decoded(package, ints):
    rows = package.shape[0]
    digits = package[rows - CODE_ROWS :, :LANES].astype(f32)
    ints[...] = (digits[0:1] * DIGIT + digits[1:2]).astype(jnp.int32)
    return lambda slot, i: ints[0, slot * FIELDS + i]


def plain(tab):
    return lambda slot, i: tab[slot, i]


def package_rows(caps, strip, frame, angles, grid):
    windows = caps * 2 * strip
    halo = angles * 2 * grid // frame
    return windows, halo


def pack_kernel(caps, tab, field, out, raw, last_rows, halo_buf, sems, row_sem):
    frame = out.shape[1]
    angles, _, strip, grid = field.shape
    at_halo, halo_rows = package_rows(caps, strip, frame, angles, grid)
    copies = window_copies(plain(tab), field, raw, sems)
    row_copy = pltpu.make_async_copy(
        field.at[:, :, pl.ds(strip - PAD, PAD), :], last_rows, row_sem.at[0]
    )
    row_copy.start()
    place = lax.broadcasted_iota(jnp.int32, (CODE_ROWS, frame), 1)
    row = lax.broadcasted_iota(jnp.int32, (CODE_ROWS, frame), 0)
    high = jnp.zeros((CODE_ROWS, frame), jnp.int32)
    low = jnp.zeros((CODE_ROWS, frame), jnp.int32)
    for slot in range(caps):
        for i in range(FIELDS):
            here = place == slot * FIELDS + i
            high = jnp.where(here, tab[slot, i] // DIGIT, high)
            low = jnp.where(here, lax.rem(tab[slot, i], DIGIT), low)
    code = jnp.where(row == 0, high, jnp.where(row == 1, low, 0))
    out[out.shape[0] - CODE_ROWS :] = code.astype(f32).astype(bf16)
    row_copy.wait()
    per_row = grid // frame
    for a in range(angles):
        for part in range(2):
            for k in range(per_row):
                i = (a * 2 + part) * per_row + k
                halo_buf[i : i + 1] = last_rows[a, part, PAD - 1 :, k * frame : (k + 1) * frame]
    left_over = halo_buf[...]
    for i in range(3):
        digit = left_over.astype(bf16)
        out[at_halo + i * halo_rows : at_halo + (i + 1) * halo_rows] = digit
        left_over = left_over - digit.astype(f32)
    for slot in range(caps):
        copies[slot][0].wait()
        for part in range(2):
            at = (slot * 2 + part) * strip
            out[at : at + strip] = window_values(copies, raw, slot, part)


def pack(tab, field, caps, frame):
    angles, _, strip, grid = field.shape
    at_halo, halo_rows = package_rows(caps, strip, frame, angles, grid)
    return pl.pallas_call(
        functools.partial(pack_kernel, caps),
        out_shape=jax.ShapeDtypeStruct((at_halo + 3 * halo_rows + CODE_ROWS, frame), bf16),
        in_specs=[SMEM_SPEC, ANY_SPEC],
        out_specs=VMEM_SPEC,
        scratch_shapes=[
            pltpu.VMEM((caps, 2, strip, frame + LANES), f32),
            pltpu.VMEM((angles, 2, PAD, grid), f32),
            pltpu.VMEM((halo_rows, frame), f32),
            pltpu.SemaphoreType.DMA((caps,)),
            pltpu.SemaphoreType.DMA((1,)),
        ],
        compiler_params=PARAMS,
        cost_estimate=cost(6),
        name="pack",
    )(tab, field)


def extract_kernel(coded, tab, field, *rest):
    raw, ints, sems = rest[-3:]
    out = rest[0] if coded else rest[1]
    read = decoded(tab, ints) if coded else plain(tab)
    copies = window_copies(read, field, raw, sems)
    for slot in range(out.shape[0]):
        copies[slot][0].wait()
        for part in range(2):
            out[slot, part] = window_values(copies, raw, slot, part)


def extract(tab, coded, field, caps, frame, package=None):
    angles, _, strip, grid = field.shape
    window = jax.ShapeDtypeStruct((caps, 2, strip, frame), bf16)
    through = [] if coded else [package]
    out = pl.pallas_call(
        functools.partial(extract_kernel, coded),
        out_shape=[window] + [jax.ShapeDtypeStruct(x.shape, x.dtype) for x in through],
        in_specs=[VMEM_SPEC if coded else SMEM_SPEC, ANY_SPEC] + [ANY_SPEC] * len(through),
        out_specs=[VMEM_SPEC] + [ANY_SPEC] * len(through),
        input_output_aliases={2: 1} if through else {},
        scratch_shapes=[
            pltpu.VMEM((caps, 2, strip, frame + LANES), f32),
            pltpu.VMEM((1, LANES), jnp.int32),
            pltpu.SemaphoreType.DMA((caps,)),
        ],
        compiler_params=PARAMS,
        cost_estimate=cost(2),
        name="extract",
    )(tab, field, *through)
    return out[0] if coded else out


def frame_kernel(reach, package, measured, probe, left, right, *rest):
    windows = rest[:reach]
    pieces = rest[reach : 2 * reach + 1]
    window_buf, update_buf, ints = rest[2 * reach + 1 :]
    caps, _, strip, frame = windows[0].shape
    read = decoded(package, ints)
    blocks = frame // LANES
    count = read(0, 3)
    probe_re, probe_im = probe[0], probe[1]
    peak = jnp.max(probe_re * probe_re + probe_im * probe_im) + epsilon_term
    for slot in range(caps):
        update_buf[...] = jnp.zeros_like(update_buf)

        @pl.when(slot < count)
        def _():
            offset = clip(read(slot, 0), strip - 1)
            for j in range(reach + 1):
                for part in range(2):
                    for k in range(blocks):
                        lanes = slice(k * LANES, (k + 1) * LANES)
                        at = (slot * 2 + part) * strip
                        values = (
                            windows[j - 1][slot, part, :, lanes]
                            if j
                            else package[at : at + strip, lanes]
                        )
                        window_buf[part, k, j * strip : (j + 1) * strip] = values.astype(f32)
            obj_re, obj_im = (
                jnp.concatenate(
                    [window_buf[part, k, pl.ds(offset, frame), :] for k in range(blocks)], axis=1
                )
                for part in range(2)
            )
            wave = jnp.concatenate(
                [
                    (probe_re * obj_re - probe_im * obj_im).astype(bf16),
                    (probe_re * obj_im + probe_im * obj_re).astype(bf16),
                ],
                axis=0,
            )

            def both(first, second, rows):
                first_half = jnp.dot(first, rows, preferred_element_type=f32).astype(bf16)
                beside = jnp.concatenate([first_half[:frame], first_half[frame:]], axis=1)
                return jnp.dot(beside, second, preferred_element_type=f32)

            spectrum = both(left[...], right[...], wave)
            spec_re, spec_im = spectrum[:, :frame], spectrum[:, frame:]
            power = spec_re * spec_re + spec_im * spec_im
            factor = (
                measured[slot].astype(f32)
                * lax.rsqrt(jnp.maximum(power, magnitude_floor**2)) - 1.0
            )
            change = jnp.concatenate(
                [(spec_re * factor).astype(bf16), (spec_im * factor).astype(bf16)], axis=0
            )
            correction = both(right[...], left[...], change)
            corr_re, corr_im = correction[:, :frame], correction[:, frame:]
            update = (
                (probe_re * corr_re + probe_im * corr_im) / peak,
                (probe_re * corr_im - probe_im * corr_re) / peak,
            )
            for part in range(2):
                for k in range(blocks):
                    update_buf[part, k, pl.ds(2 * PAD + offset, frame), :] = update[part][
                        :, k * LANES : (k + 1) * LANES
                    ]

        for part in range(2):
            for k in range(blocks):
                lanes = slice(k * LANES, (k + 1) * LANES)
                for j in range(reach + 1):
                    pieces[j][slot, part, :, lanes] = update_buf[
                        part, k, j * strip + PAD : (j + 1) * strip + 3 * PAD
                    ].astype(pieces[j].dtype)


def run_frames(package, measured, probe, windows, center):
    reach = len(windows)
    caps, _, strip, frame = windows[0].shape
    left, right = fourier_blocks(frame)
    rows = (reach + 1) * strip
    piece = lambda j: jax.ShapeDtypeStruct(
        (caps, 2, strip + 2 * PAD, frame), f32 if j == center else bf16
    )
    return pl.pallas_call(
        functools.partial(frame_kernel, reach),
        out_shape=[piece(j) for j in range(reach + 1)],
        in_specs=[VMEM_SPEC] * (5 + reach),
        out_specs=[VMEM_SPEC] * (reach + 1),
        scratch_shapes=[
            pltpu.VMEM((2, frame // LANES, rows, LANES), f32),
            pltpu.VMEM((2, frame // LANES, rows + 4 * PAD, LANES), f32),
            pltpu.VMEM((1, LANES), jnp.int32),
        ],
        compiler_params=PARAMS,
        cost_estimate=cost(5),
        name="frames",
    )(package, measured, probe, jnp.asarray(left), jnp.asarray(right), *windows)


def reversed_lanes(values):
    index = LANES - 1 - lax.broadcasted_iota(jnp.int32, values.shape, 1)
    return jnp.take_along_axis(values, index, axis=1)


def split_pair(values):
    high = values.astype(bf16)
    return high, (values - high.astype(f32)).astype(bf16)


def three_pass(rows, count, high, low):
    both = jnp.dot(rows, high, preferred_element_type=f32)
    return both[:count] + both[count:] + jnp.dot(rows[:count], low, preferred_element_type=f32)


def update_kernel(reach, center, *refs):
    tabs = refs[:reach]
    field, package, halo, scan, segs, tables, *rest = refs[reach:]
    tabs = tabs[:center] + (None,) + tabs[center:]
    pieces = rest[: reach + 1]
    updated, inner, carry_y, carry_z, ends = rest[reach + 1 : reach + 6]
    ext, col_bond, source, edge, rows_in, ints, table, load_sems, store_sems, table_sems = rest[reach + 6 :]
    angles, _, strip, grid = field.shape
    blocks = grid // LANES
    half_blocks = blocks // 2
    half = grid // 2
    steps = strip // SEG
    count = angles * strip + 2 * PAD
    caps = pieces[0].shape[0]
    frame = pieces[0].shape[3]
    frame_blocks = frame // LANES

    def load(a, b):
        start = b * LANES
        return pltpu.make_async_copy(
            field.at[a, :, :, pl.ds(start, LANES)],
            ext.at[a, :, b, pl.ds(PAD, strip), :],
            load_sems.at[a, b],
        )

    def store(a, b):
        start = b * LANES
        return pltpu.make_async_copy(
            ext.at[a, :, b, pl.ds(PAD, strip), :],
            updated.at[a, :, :, pl.ds(start, LANES)],
            store_sems.at[a, b],
        )

    def load_table(h, k):
        return pltpu.make_async_copy(
            tables.at[0, k, h], table.at[k, h], table_sems.at[k, h]
        )

    for a in range(angles):
        for b in range(blocks):
            load(a, b).start()
    for h in range(2):
        for k in range(2):
            load_table(h, k).start()

    halo_rows = halo.shape[0] // 3
    top = sum(halo[i * halo_rows : (i + 1) * halo_rows].astype(f32) for i in range(3))
    per_row = grid // frame
    read = decoded(package, ints)
    for a in range(angles):
        for part in range(2):
            for b in range(blocks):
                row = (a * 2 + part) * per_row + b // frame_blocks
                lanes = slice(b % frame_blocks * LANES, (b % frame_blocks + 1) * LANES)
                ext[a, part, b, PAD - 1 : PAD, :] = top[row : row + 1, lanes]
            ext[a, part, blocks] = jnp.zeros((strip + 2 * PAD, LANES), f32)
    for a in range(angles):
        for b in range(blocks):
            load(a, b).wait()

    rows = strip + 2 * PAD

    def add_piece(piece, tab, slot):
        @pl.when(slot < tab(0, 3))
        def _():
            column = clip(tab(slot, 1), grid - frame)
            angle = clip(tab(slot, 2), angles - 1)
            block = jnp.minimum(column // LANES, blocks - frame_blocks - 1)
            shift = column - block * LANES
            for part in range(2):
                values = piece[slot, part].astype(f32)
                values = jnp.concatenate([values, jnp.zeros((rows, LANES), f32)], axis=1)
                values = pltpu.roll(values, shift, axis=1)
                for k in range(frame_blocks + 1):
                    spot = ext.at[angle, part, block + k]
                    spot[...] += values[:, k * LANES : (k + 1) * LANES]

    for slot in range(caps):
        for j in range(reach + 1):
            add_piece(pieces[j], read if j == center else plain(tabs[j]), slot)

    for a in range(angles):
        for b in range(blocks):
            store(a, b).start()

    lane = lax.broadcasted_iota(jnp.int32, (SEG, LANES), 1)
    sub = lax.broadcasted_iota(jnp.int32, (SEG, LANES), 0)

    def power_of(re, im):
        return re * re + (im * im + 0.5 * soften_term)

    def bond(re, im, power, re_to, im_to):
        return (re * im_to - im * re_to) * pl.reciprocal(
            power + power_of(re_to, im_to), approx=True
        )

    for a in range(angles):
        col_bond[...] = jnp.zeros_like(col_bond)

        def columns(b, _, a=a):
            def cells(first, block):
                return ext[a, 0, block, first : first + SEG], ext[a, 1, block, first : first + SEG]

            groups = strip // SEG
            re, im = cells(0, b)
            above = bond(re, im, power_of(re, im), *cells(1, b))
            edge[a, b] = -above[SEG - 1 :]
            batch = min(BATCH, groups)
            for g0 in range(0, groups, batch):
                firsts = [PAD + (g0 + i) * SEG for i in range(batch)]
                here = [cells(first, b) for first in firsts]
                to_right = [
                    [
                        pltpu.roll(jnp.where(lane == 0, after, now), LANES - 1, axis=1)
                        for now, after in zip(here[i], cells(firsts[i], b + 1))
                    ]
                    for i in range(batch)
                ]
                powers = [power_of(*here[i]) for i in range(batch)]
                downs = [bond(*here[i], powers[i], *cells(firsts[i] + 1, b)) for i in range(batch)]
                if g0 + batch == groups:
                    downs[-1] = jnp.where(sub == SEG - 1, 0.0, downs[-1])
                rights = [bond(*here[i], powers[i], *to_right[i]) for i in range(batch)]
                rows = [slice((g0 + i) * SEG, (g0 + i + 1) * SEG) for i in range(batch)]
                from_left = [
                    pltpu.roll(
                        jnp.where(lane == LANES - 1, col_bond[rows[i]], rights[i]), 1, axis=1
                    )
                    for i in range(batch)
                ]
                values = []
                for i in range(batch):
                    from_above = pltpu.roll(
                        jnp.where(sub == SEG - 1, above, downs[i]), 1, axis=0
                    )
                    above = downs[i]
                    values.append(from_above - downs[i] + from_left[i] - rights[i])
                for i in range(batch):
                    col_bond[rows[i]] = rights[i]
                    source[a, b, rows[i]] = values[i]
            return 0

        lax.fori_loop(0, blocks, columns, 0)

    def fold(b, _):
        lanes = pl.ds(pl.multiple_of(b * LANES, LANES), LANES)
        for a in range(angles):
            for t in range(0, steps, 2):
                lower = jnp.concatenate(
                    [source[a, b, pl.ds(t + i, SEG, stride=steps), :] for i in range(2)], 0
                )
                upper = jnp.concatenate(
                    [
                        source[a, blocks - 1 - b, pl.ds(t + i, SEG, stride=steps), :]
                        for i in range(2)
                    ],
                    0,
                )
                upper = reversed_lanes(upper)
                at = a * strip + t * SEG
                for h, values in enumerate((lower + upper, lower - upper)):
                    high, low = split_pair(values)
                    rows_in[h, at : at + 2 * SEG, lanes] = high
                    rows_in[h, count + at : count + at + 2 * SEG, lanes] = low
        edges = [jnp.concatenate([edge[a, i] for a in range(angles)], 0) for i in (b, blocks - 1 - b)]
        fill = jnp.zeros((2 * PAD - angles, LANES), f32)
        lower, upper = (jnp.concatenate([rows, fill], 0) for rows in edges)
        upper = reversed_lanes(upper)
        at = angles * strip
        for h, values in enumerate((lower + upper, lower - upper)):
            high, low = split_pair(values)
            rows_in[h, at : at + 2 * PAD, lanes] = high
            rows_in[h, count + at : count + at + 2 * PAD, lanes] = low
        return 0

    lax.fori_loop(0, half_blocks, fold, 0)

    wide = min(2 * LANES, half)
    sub = lax.broadcasted_iota(jnp.int32, (SEG, wide), 0)
    for h in range(2):
        for k in range(2):
            load_table(h, k).wait()

        def transform(c, _, h=h):
            lanes = pl.ds(pl.multiple_of(c * wide, wide), wide)
            spots = pl.ds(pl.multiple_of(h * half + c * wide, wide), wide)
            values = three_pass(rows_in[h], count, table[0, h, :, lanes], table[1, h, :, lanes])
            root = jnp.broadcast_to(scan[0:1, spots], (SEG, wide))
            for a in range(angles):
                terms = [
                    values[a * strip + t * SEG : a * strip + (t + 1) * SEG] for t in range(steps)
                ]
                down = [terms[0]]
                for t in range(1, steps):
                    down.append(terms[t] + root * down[-1])
                up = terms[steps - 1]
                inner[a, (steps - 1) * SEG : steps * SEG, spots] = down[steps - 1]
                for t in range(steps - 2, -1, -1):
                    after = root * up
                    inner[a, t * SEG : (t + 1) * SEG, spots] = down[t] + after
                    up = terms[t] + after
                tail_y, tail_z = down[steps - 1], up
                for i, k in enumerate((1, 2, 4)):
                    factor = scan[i + 1 : i + 2, spots]
                    tail_y = tail_y + jnp.where(
                        sub >= k, factor * pltpu.roll(tail_y, k, axis=0), 0.0
                    )
                    tail_z = tail_z + jnp.where(
                        sub < SEG - k, factor * pltpu.roll(tail_z, SEG - k, axis=0), 0.0
                    )
                above = values[angles * strip + a : angles * strip + a + 1]
                carry_y[a, :, spots] = (
                    jnp.where(sub >= 1, pltpu.roll(tail_y, 1, axis=0), 0.0) + segs[:, spots] * above
                )
                carry_z[a, :, spots] = jnp.where(
                    sub < SEG - 1, pltpu.roll(tail_z, SEG - 1, axis=0), 0.0
                )
                ends[0, a : a + 1, spots] = tail_z[0:1] + scan[5:6, spots] * above
                ends[1, a : a + 1, spots] = tail_y[SEG - 1 : SEG] + scan[6:7, spots] * above
            return 0

        lax.fori_loop(0, half // wide, transform, 0)

    for a in range(angles):
        for b in range(blocks):
            store(a, b).wait()


def run_update(tabs, field, package, halo, scan, segs, tables, pieces, center):
    angles, _, strip, grid = field.shape
    reach = len(pieces) - 1
    blocks = grid // LANES
    half = grid // 2
    return pl.pallas_call(
        functools.partial(update_kernel, reach, center),
        out_shape=[
            jax.ShapeDtypeStruct(field.shape, f32),
            jax.ShapeDtypeStruct((angles, strip, grid), f32),
            jax.ShapeDtypeStruct((angles, SEG, grid), f32),
            jax.ShapeDtypeStruct((angles, SEG, grid), f32),
            jax.ShapeDtypeStruct((2, angles, grid), f32),
        ],
        in_specs=[SMEM_SPEC] * reach
        + [ANY_SPEC]
        + [VMEM_SPEC] * 4
        + [ANY_SPEC]
        + [VMEM_SPEC] * (reach + 1),
        out_specs=[ANY_SPEC] + [VMEM_SPEC] * 4,
        scratch_shapes=[
            pltpu.VMEM((angles, 2, blocks + 1, strip + 2 * PAD, LANES), f32),
            pltpu.VMEM((strip, LANES), f32),
            pltpu.VMEM((angles, blocks, strip, LANES), f32),
            pltpu.VMEM((angles, blocks, 1, LANES), f32),
            pltpu.VMEM((2, 2 * (angles * strip + 2 * PAD), half), bf16),
            pltpu.VMEM((1, LANES), jnp.int32),
            pltpu.VMEM(tables.shape[1:], bf16),
            pltpu.SemaphoreType.DMA((angles, blocks)),
            pltpu.SemaphoreType.DMA((angles, blocks)),
            pltpu.SemaphoreType.DMA((2, 2)),
        ],
        compiler_params=UPDATE_PARAMS,
        cost_estimate=cost(14),
        name="update",
    )(*tabs, field, package, halo, scan, segs, tables, *pieces)


def phase_kernel(inner, carry_y, carry_z, enter, scan, powers, segs, segs_back, tables, out_hbm, rest, rows_in, table, out, table_sems, out_sems):
    angles, strip, grid = inner.shape
    half = grid // 2
    steps = strip // SEG
    count = angles * strip
    half_blocks = half // LANES
    wide = min(2 * LANES, half)
    chunks = half // wide

    def load_table(c):
        lanes = pl.ds(pl.multiple_of(c * wide, wide), wide)
        return pltpu.make_async_copy(
            tables.at[1, :, :, :, lanes], table.at[:, :, :, lanes], table_sems.at[c]
        )

    def store(c, side):
        start = c * wide if side == 0 else grid - (c + 1) * wide
        lanes = pl.ds(pl.multiple_of(start, wide), wide)
        return pltpu.make_async_copy(
            out.at[:, :, lanes], out_hbm.at[:, :, lanes], out_sems.at[c, side]
        )

    for c in range(chunks):
        load_table(c).start()

    def solve(b, _):
        spots = pl.ds(pl.multiple_of(b * LANES, LANES), LANES)
        scale = scan[4:5, spots]
        for a in range(angles):
            from_y = scale * (carry_y[a, :, spots] + segs[:, spots] * enter[0, a : a + 1, spots])
            from_z = scale * (carry_z[a, :, spots] + segs_back[:, spots] * enter[1, a : a + 1, spots])
            for t in range(steps):
                rest[a, b, pl.ds(t, SEG, stride=steps), :] = (
                    scale * inner[a, t * SEG : (t + 1) * SEG, spots]
                    + powers[t : t + 1, spots] * from_y
                    + powers[steps - 1 - t : steps - t, spots] * from_z
                )
        return 0

    lax.fori_loop(0, 2 * half_blocks, solve, 0)

    def split(b, _):
        lanes = pl.ds(pl.multiple_of(b * LANES, LANES), LANES)
        for h in range(2):
            for a in range(angles):
                high, low = split_pair(rest[a, h * half_blocks + b])
                rows_in[h, a * strip : (a + 1) * strip, lanes] = high
                rows_in[h, count + a * strip : count + (a + 1) * strip, lanes] = low
        return 0

    lax.fori_loop(0, half_blocks, split, 0)

    def back(c, _):
        lanes = pl.ds(pl.multiple_of(c * wide, wide), wide)
        load_table(c).wait()
        even, odd = (
            three_pass(rows_in[h], count, table[0, h, :, lanes], table[1, h, :, lanes])
            for h in range(2)
        )
        mirrored = even - odd
        plain = even + odd
        for a in range(angles):
            out[a, :, lanes] = plain[a * strip : (a + 1) * strip]
            for k in range(wide // LANES):
                spot = pl.ds(
                    pl.multiple_of(grid - (k + 1) * LANES - c * wide, LANES), LANES
                )
                out[a, :, spot] = reversed_lanes(
                    mirrored[a * strip : (a + 1) * strip, k * LANES : (k + 1) * LANES]
                )
        for side in range(2):
            store(c, side).start()
        return 0

    lax.fori_loop(0, chunks, back, 0)
    for c in range(chunks):
        for side in range(2):
            store(c, side).wait()


def run_phase(inner, carry_y, carry_z, enter, scan, powers, segs, segs_back, tables):
    angles, strip, grid = inner.shape
    half = grid // 2
    chunks = half // min(2 * LANES, half)
    return pl.pallas_call(
        phase_kernel,
        out_shape=jax.ShapeDtypeStruct((angles, strip, grid), f32),
        in_specs=[VMEM_SPEC] * 8 + [ANY_SPEC],
        out_specs=ANY_SPEC,
        scratch_shapes=[
            pltpu.VMEM((angles, grid // LANES, strip, LANES), f32),
            pltpu.VMEM((2, 2 * angles * strip, half), bf16),
            pltpu.VMEM(tables.shape[1:], bf16),
            pltpu.VMEM((angles, strip, grid), f32),
            pltpu.SemaphoreType.DMA((chunks,)),
            pltpu.SemaphoreType.DMA((chunks, 2)),
        ],
        compiler_params=PHASE_PARAMS,
        cost_estimate=cost(7),
        name="phase",
    )(inner, carry_y, carry_z, enter, scan, powers, segs, segs_back, tables)


def passed_along(x, by):
    size = lax.axis_size("tile")
    pairs = [(i, i + by) for i in range(size) if 0 <= i + by < size]
    return lax.ppermute(x, "tile", pairs)


def entering_values(ends, strips, closing):
    size = lax.axis_size("tile")
    me = lax.axis_index("tile")
    head, tail = ends[0], ends[1]
    enter_y = jnp.zeros_like(head)
    enter_z = jnp.zeros_like(head)
    row = lambda i: lax.dynamic_slice_in_dim(strips, i, 1, 0)
    width = 1
    while width < size:
        other = lax.ppermute(
            jnp.stack([head, tail]), "tile", [(i, i ^ width) for i in range(size)]
        )
        head_to, tail_to = other[0], other[1]
        second = (me & width) != 0
        before = me & (width - 1)
        span = strips[width : width + 1]
        enter_y = enter_y + jnp.where(second, row(before) * tail_to, 0.0)
        enter_z = enter_z + jnp.where(second, 0.0, row(width - 1 - before) * head_to)
        head, tail = (
            jnp.where(second, head_to + span * head, head + span * head_to),
            jnp.where(second, tail + span * tail_to, tail_to + span * tail),
        )
        width *= 2
    whole = strips[size : size + 1]
    enter_y = enter_y + row(me) * (head + whole * tail) * closing
    enter_z = enter_z + row(size - 1 - me) * (tail + whole * head) * closing
    return jnp.stack([enter_y, enter_z])


def body(object_field, probe, measured, frame_table, frame_count):
    angles, _, strip, grid = object_field.shape
    caps, frame = measured.shape[0], measured.shape[1]
    reach = frame // strip
    center = reach // 2
    halves = cosine_halves(grid)
    tables = jnp.asarray(np.stack([split_table(np.swapaxes(halves, 1, 2)), split_table(halves)]))
    scan, powers, segs, segs_back, strips, closing = (
        jnp.asarray(x) for x in decay_tables(grid, strip)
    )

    own_tab = jnp.concatenate(
        [frame_table, jnp.broadcast_to(frame_count[None, :], (caps, 1))], axis=1
    )
    far = [j for j in range(1, reach + 1) if j != center]
    tabs = {0: own_tab}
    for j in far:
        tabs[j] = passed_along(own_tab, j)
    measured_here = passed_along(measured, center)
    package = pack(own_tab, object_field, caps, frame)
    windows = {}
    for j in far:
        window, package = extract(tabs[j], False, object_field, caps, frame, package)
        windows[j] = passed_along(window, center - j)
    arrived = passed_along(package, center)
    at_halo, halo_rows = package_rows(caps, strip, frame, angles, grid)
    halo = slice(at_halo, at_halo + 3 * halo_rows)
    top = arrived[halo] if center == 1 else passed_along(package[halo], 1)
    windows[center] = extract(arrived, True, object_field, caps, frame)
    pieces = run_frames(arrived, measured_here, probe, [windows[j] for j in range(1, reach + 1)], center)
    pieces = [
        piece if j == center else passed_along(piece, j - center) for j, piece in enumerate(pieces)
    ]
    updated, inner, carry_y, carry_z, ends = run_update(
        [tabs[j] for j in range(reach + 1) if j != center],
        object_field,
        arrived,
        top,
        scan,
        segs,
        tables,
        pieces,
        center,
    )
    enter = entering_values(ends, strips, closing)
    phase_map = run_phase(
        inner, carry_y, carry_z, enter, scan, powers, segs, segs_back, tables
    )
    return (updated, phase_map)


def solution(mesh):
    return jax.shard_map(
        body,
        mesh=mesh,
        in_specs=(
            P("group", None, "tile", None),
            P(),
            P(("group", "tile"), None, None),
            P(("group", "tile"), None),
            P(("group", "tile")),
        ),
        out_specs=(P("group", None, "tile", None), P("group", "tile", None)),
        check_vma=False,
    )
```

```python
import functools
import math

import jax
import jax.numpy as jnp
import ml_dtypes
import numpy as np
from jax import lax
from jax.experimental import pallas as pl
from jax.experimental.pallas import tpu as pltpu
from jax.sharding import PartitionSpec as P

magnitude_floor = 0.5
soften_term = 0.5
screen_term = 0.0001
epsilon_term = 1e-06
LANES = 128
SEG = 8
PAD = 8
f32 = jnp.float32
bf16 = jnp.bfloat16
VMEM_SPEC = pl.BlockSpec(memory_space=pltpu.VMEM)
SMEM_SPEC = pl.BlockSpec(memory_space=pltpu.SMEM)
ANY_SPEC = pl.BlockSpec(memory_space=pl.ANY)
PARAMS = pltpu.CompilerParams(vmem_limit_bytes=26 * 1024 * 1024)
UPDATE_PARAMS = pltpu.CompilerParams(vmem_limit_bytes=32 * 1024 * 1024)
PHASE_PARAMS = pltpu.CompilerParams(vmem_limit_bytes=46 * 1024 * 1024)
DIGIT = 64
CODE_ROWS = 16
FIELDS = 4
BATCH = 16


def cost(micros):
    return pl.CostEstimate(flops=0, bytes_accessed=int(micros * 3.0e6), transcendentals=0)


def split_table(table):
    high = table.astype(ml_dtypes.bfloat16)
    low = (table - high.astype(np.float64)).astype(ml_dtypes.bfloat16)
    return np.stack([high, low])


def fourier_blocks(side):
    index = np.arange(side)
    phase = (index[:, None] * index[None, :] % side) * (-2.0 * math.pi / side)
    cos_part = np.cos(phase) / math.sqrt(side)
    sin_part = np.sin(phase) / math.sqrt(side)
    left = np.block([[cos_part, -sin_part], [sin_part, cos_part]])
    right = np.block([[cos_part, sin_part], [-sin_part, cos_part]])
    return left.astype(ml_dtypes.bfloat16), right.astype(ml_dtypes.bfloat16)


def cosine_halves(grid):
    half = grid // 2
    freqs = np.arange(grid)
    pixels = np.arange(half)
    phase = (2 * pixels[None, :] + 1) * freqs[:, None] % (4 * grid)
    scale = np.where(freqs == 0, math.sqrt(1.0 / grid), math.sqrt(2.0 / grid))
    table = scale[:, None] * np.cos(phase * (math.pi / (2 * grid)))
    return np.stack([table[0::2], table[1::2]])


def decay_tables(grid, strip):
    freqs = np.concatenate([np.arange(0, grid, 2), np.arange(1, grid, 2)])
    mu = screen_term + 4.0 * np.sin(freqs * (math.pi / (2 * grid))) ** 2
    root = 1.0 + mu / 2 - np.sqrt(mu + mu * mu / 4)
    log_root = np.log(root)
    steps = strip // SEG
    devices = grid // strip

    def power(exponents):
        return np.exp(np.maximum(log_root[None, :] * np.asarray(exponents)[:, None], -80.0)) * (
            log_root[None, :] * np.asarray(exponents)[:, None] > -80.0
        )

    scan = np.concatenate(
        [
            power([1, steps, 2 * steps, 4 * steps]),
            (2 * root / (1 - root * root))[None],
            (1 / root)[None],
            power([strip]),
        ]
    )
    inner = power(np.arange(1, steps + 1))
    segs = power(steps * np.arange(SEG))
    strips = power(strip * np.arange(devices + 1))
    closing = 1.0 / (1.0 - power([2 * grid]))
    as32 = lambda x: x.astype(np.float32)
    return as32(scan), as32(inner), as32(segs), as32(segs[::-1]), as32(strips), as32(closing)


def clip(value, top):
    return jnp.minimum(jnp.maximum(value, 0), top)


def window_copies(tab, field, raw, sems):
    caps, wide = raw.shape[0], raw.shape[3]
    frame = wide - LANES
    angles, grid = field.shape[0], field.shape[3]
    copies = []
    for slot in range(caps):
        column = clip(tab(slot, 1), grid - frame)
        angle = clip(tab(slot, 2), angles - 1)
        block = jnp.minimum(column // LANES, (grid - wide) // LANES)
        start = pl.multiple_of(block * LANES, LANES)
        copy = pltpu.make_async_copy(
            field.at[angle, :, :, pl.ds(start, wide)], raw.at[slot], sems.at[slot]
        )
        copy.start()
        copies.append((copy, lax.rem(wide - (column - block * LANES), wide)))
    return copies


def window_values(copies, raw, slot, part):
    wide = raw.shape[3]
    return pltpu.roll(raw[slot, part], copies[slot][1], axis=1)[:, : wide - LANES].astype(bf16)


def decoded(package, ints):
    rows = package.shape[0]
    digits = package[rows - CODE_ROWS :, :LANES].astype(f32)
    ints[...] = (digits[0:1] * DIGIT + digits[1:2]).astype(jnp.int32)
    return lambda slot, i: ints[0, slot * FIELDS + i]


def plain(tab):
    return lambda slot, i: tab[slot, i]


def package_rows(caps, strip, frame, angles, grid):
    windows = caps * 2 * strip
    halo = angles * 2 * grid // frame
    return windows, halo


def pack_kernel(caps, tab, field, out, raw, last_rows, halo_buf, sems, row_sem):
    frame = out.shape[1]
    angles, _, strip, grid = field.shape
    at_halo, halo_rows = package_rows(caps, strip, frame, angles, grid)
    copies = window_copies(plain(tab), field, raw, sems)
    row_copy = pltpu.make_async_copy(
        field.at[:, :, pl.ds(strip - PAD, PAD), :], last_rows, row_sem.at[0]
    )
    row_copy.start()
    place = lax.broadcasted_iota(jnp.int32, (CODE_ROWS, frame), 1)
    row = lax.broadcasted_iota(jnp.int32, (CODE_ROWS, frame), 0)
    high = jnp.zeros((CODE_ROWS, frame), jnp.int32)
    low = jnp.zeros((CODE_ROWS, frame), jnp.int32)
    for slot in range(caps):
        for i in range(FIELDS):
            here = place == slot * FIELDS + i
            high = jnp.where(here, tab[slot, i] // DIGIT, high)
            low = jnp.where(here, lax.rem(tab[slot, i], DIGIT), low)
    code = jnp.where(row == 0, high, jnp.where(row == 1, low, 0))
    out[out.shape[0] - CODE_ROWS :] = code.astype(f32).astype(bf16)
    row_copy.wait()
    per_row = grid // frame
    for a in range(angles):
        for part in range(2):
            for k in range(per_row):
                i = (a * 2 + part) * per_row + k
                halo_buf[i : i + 1] = last_rows[a, part, PAD - 1 :, k * frame : (k + 1) * frame]
    left_over = halo_buf[...]
    for i in range(3):
        digit = left_over.astype(bf16)
        out[at_halo + i * halo_rows : at_halo + (i + 1) * halo_rows] = digit
        left_over = left_over - digit.astype(f32)
    for slot in range(caps):
        copies[slot][0].wait()
        for part in range(2):
            at = (slot * 2 + part) * strip
            out[at : at + strip] = window_values(copies, raw, slot, part)


def pack(tab, field, caps, frame):
    angles, _, strip, grid = field.shape
    at_halo, halo_rows = package_rows(caps, strip, frame, angles, grid)
    return pl.pallas_call(
        functools.partial(pack_kernel, caps),
        out_shape=jax.ShapeDtypeStruct((at_halo + 3 * halo_rows + CODE_ROWS, frame), bf16),
        in_specs=[SMEM_SPEC, ANY_SPEC],
        out_specs=VMEM_SPEC,
        scratch_shapes=[
            pltpu.VMEM((caps, 2, strip, frame + LANES), f32),
            pltpu.VMEM((angles, 2, PAD, grid), f32),
            pltpu.VMEM((halo_rows, frame), f32),
            pltpu.SemaphoreType.DMA((caps,)),
            pltpu.SemaphoreType.DMA((1,)),
        ],
        compiler_params=PARAMS,
        cost_estimate=cost(6),
        name="pack",
    )(tab, field)


def extract_kernel(coded, tab, field, *rest):
    raw, ints, sems = rest[-3:]
    out = rest[0] if coded else rest[1]
    read = decoded(tab, ints) if coded else plain(tab)
    copies = window_copies(read, field, raw, sems)
    for slot in range(out.shape[0]):
        copies[slot][0].wait()
        for part in range(2):
            out[slot, part] = window_values(copies, raw, slot, part)


def extract(tab, coded, field, caps, frame, package=None):
    angles, _, strip, grid = field.shape
    window = jax.ShapeDtypeStruct((caps, 2, strip, frame), bf16)
    through = [] if coded else [package]
    out = pl.pallas_call(
        functools.partial(extract_kernel, coded),
        out_shape=[window] + [jax.ShapeDtypeStruct(x.shape, x.dtype) for x in through],
        in_specs=[VMEM_SPEC if coded else SMEM_SPEC, ANY_SPEC] + [ANY_SPEC] * len(through),
        out_specs=[VMEM_SPEC] + [ANY_SPEC] * len(through),
        input_output_aliases={2: 1} if through else {},
        scratch_shapes=[
            pltpu.VMEM((caps, 2, strip, frame + LANES), f32),
            pltpu.VMEM((1, LANES), jnp.int32),
            pltpu.SemaphoreType.DMA((caps,)),
        ],
        compiler_params=PARAMS,
        cost_estimate=cost(2),
        name="extract",
    )(tab, field, *through)
    return out[0] if coded else out


def frame_kernel(reach, package, measured, probe, left, right, *rest):
    windows = rest[:reach]
    pieces = rest[reach : 2 * reach + 1]
    window_buf, update_buf, ints = rest[2 * reach + 1 :]
    caps, _, strip, frame = windows[0].shape
    read = decoded(package, ints)
    blocks = frame // LANES
    count = read(0, 3)
    probe_re, probe_im = probe[0], probe[1]
    peak = jnp.max(probe_re * probe_re + probe_im * probe_im) + epsilon_term
    for slot in range(caps):
        update_buf[...] = jnp.zeros_like(update_buf)

        @pl.when(slot < count)
        def _():
            offset = clip(read(slot, 0), strip - 1)
            for j in range(reach + 1):
                for part in range(2):
                    for k in range(blocks):
                        lanes = slice(k * LANES, (k + 1) * LANES)
                        at = (slot * 2 + part) * strip
                        values = (
                            windows[j - 1][slot, part, :, lanes]
                            if j
                            else package[at : at + strip, lanes]
                        )
                        window_buf[part, k, j * strip : (j + 1) * strip] = values.astype(f32)
            obj_re, obj_im = (
                jnp.concatenate(
                    [window_buf[part, k, pl.ds(offset, frame), :] for k in range(blocks)], axis=1
                )
                for part in range(2)
            )
            wave = jnp.concatenate(
                [
                    (probe_re * obj_re - probe_im * obj_im).astype(bf16),
                    (probe_re * obj_im + probe_im * obj_re).astype(bf16),
                ],
                axis=0,
            )

            def both(first, second, rows):
                first_half = jnp.dot(first, rows, preferred_element_type=f32).astype(bf16)
                beside = jnp.concatenate([first_half[:frame], first_half[frame:]], axis=1)
                return jnp.dot(beside, second, preferred_element_type=f32)

            spectrum = both(left[...], right[...], wave)
            spec_re, spec_im = spectrum[:, :frame], spectrum[:, frame:]
            power = spec_re * spec_re + spec_im * spec_im
            factor = (
                measured[slot].astype(f32)
                * lax.rsqrt(jnp.maximum(power, magnitude_floor**2)) - 1.0
            )
            change = jnp.concatenate(
                [(spec_re * factor).astype(bf16), (spec_im * factor).astype(bf16)], axis=0
            )
            correction = both(right[...], left[...], change)
            corr_re, corr_im = correction[:, :frame], correction[:, frame:]
            update = (
                (probe_re * corr_re + probe_im * corr_im) / peak,
                (probe_re * corr_im - probe_im * corr_re) / peak,
            )
            for part in range(2):
                for k in range(blocks):
                    update_buf[part, k, pl.ds(2 * PAD + offset, frame), :] = update[part][
                        :, k * LANES : (k + 1) * LANES
                    ]

        for part in range(2):
            for k in range(blocks):
                lanes = slice(k * LANES, (k + 1) * LANES)
                for j in range(reach + 1):
                    pieces[j][slot, part, :, lanes] = update_buf[
                        part, k, j * strip + PAD : (j + 1) * strip + 3 * PAD
                    ].astype(pieces[j].dtype)


def run_frames(package, measured, probe, windows, center):
    reach = len(windows)
    caps, _, strip, frame = windows[0].shape
    left, right = fourier_blocks(frame)
    rows = (reach + 1) * strip
    piece = lambda j: jax.ShapeDtypeStruct(
        (caps, 2, strip + 2 * PAD, frame), f32 if j == center else bf16
    )
    return pl.pallas_call(
        functools.partial(frame_kernel, reach),
        out_shape=[piece(j) for j in range(reach + 1)],
        in_specs=[VMEM_SPEC] * (5 + reach),
        out_specs=[VMEM_SPEC] * (reach + 1),
        scratch_shapes=[
            pltpu.VMEM((2, frame // LANES, rows, LANES), f32),
            pltpu.VMEM((2, frame // LANES, rows + 4 * PAD, LANES), f32),
            pltpu.VMEM((1, LANES), jnp.int32),
        ],
        compiler_params=PARAMS,
        cost_estimate=cost(5),
        name="frames",
    )(package, measured, probe, jnp.asarray(left), jnp.asarray(right), *windows)


def reversed_lanes(values):
    index = LANES - 1 - lax.broadcasted_iota(jnp.int32, values.shape, 1)
    return jnp.take_along_axis(values, index, axis=1)


def split_pair(values):
    high = values.astype(bf16)
    return high, (values - high.astype(f32)).astype(bf16)


def three_pass(rows, count, high, low):
    both = jnp.dot(rows, high, preferred_element_type=f32)
    return both[:count] + both[count:] + jnp.dot(rows[:count], low, preferred_element_type=f32)


def update_kernel(reach, center, *refs):
    tabs = refs[:reach]
    field, package, halo, scan, segs, table, *rest = refs[reach:]
    tabs = tabs[:center] + (None,) + tabs[center:]
    pieces = rest[: reach + 1]
    updated, inner, carry_y, carry_z, ends = rest[reach + 1 : reach + 6]
    ext, col_bond, source, edge, rows_in, ints, load_sems, store_sems = rest[reach + 6 :]
    angles, _, strip, grid = field.shape
    blocks = grid // LANES
    half_blocks = blocks // 2
    half = grid // 2
    steps = strip // SEG
    count = angles * strip + 2 * PAD
    caps = pieces[0].shape[0]
    frame = pieces[0].shape[3]
    frame_blocks = frame // LANES

    def load(a, b):
        start = b * LANES
        return pltpu.make_async_copy(
            field.at[a, :, :, pl.ds(start, LANES)],
            ext.at[a, :, b, pl.ds(PAD, strip), :],
            load_sems.at[a, b],
        )

    def store(a, b):
        start = b * LANES
        return pltpu.make_async_copy(
            ext.at[a, :, b, pl.ds(PAD, strip), :],
            updated.at[a, :, :, pl.ds(start, LANES)],
            store_sems.at[a, b],
        )

    for a in range(angles):
        for b in range(blocks):
            load(a, b).start()
    halo_rows = halo.shape[0] // 3
    top = sum(halo[i * halo_rows : (i + 1) * halo_rows].astype(f32) for i in range(3))
    per_row = grid // frame
    read = decoded(package, ints)
    for a in range(angles):
        for part in range(2):
            for b in range(blocks):
                row = (a * 2 + part) * per_row + b // frame_blocks
                lanes = slice(b % frame_blocks * LANES, (b % frame_blocks + 1) * LANES)
                ext[a, part, b, PAD - 1 : PAD, :] = top[row : row + 1, lanes]
            ext[a, part, blocks] = jnp.zeros((strip + 2 * PAD, LANES), f32)
    for a in range(angles):
        for b in range(blocks):
            load(a, b).wait()

    rows = strip + 2 * PAD

    def add_piece(piece, tab, slot):
        @pl.when(slot < tab(0, 3))
        def _():
            column = clip(tab(slot, 1), grid - frame)
            angle = clip(tab(slot, 2), angles - 1)
            block = jnp.minimum(column // LANES, blocks - frame_blocks - 1)
            shift = column - block * LANES
            for part in range(2):
                values = piece[slot, part].astype(f32)
                values = jnp.concatenate([values, jnp.zeros((rows, LANES), f32)], axis=1)
                values = pltpu.roll(values, shift, axis=1)
                for k in range(frame_blocks + 1):
                    spot = ext.at[angle, part, block + k]
                    spot[...] += values[:, k * LANES : (k + 1) * LANES]

    for slot in range(caps):
        for j in range(reach + 1):
            add_piece(pieces[j], read if j == center else plain(tabs[j]), slot)

    for a in range(angles):
        for b in range(blocks):
            store(a, b).start()

    lane = lax.broadcasted_iota(jnp.int32, (SEG, LANES), 1)
    sub = lax.broadcasted_iota(jnp.int32, (SEG, LANES), 0)

    def power_of(re, im):
        return re * re + (im * im + 0.5 * soften_term)

    def bond(re, im, power, re_to, im_to):
        return (re * im_to - im * re_to) * pl.reciprocal(
            power + power_of(re_to, im_to), approx=True
        )

    for a in range(angles):
        col_bond[...] = jnp.zeros_like(col_bond)

        def columns(b, _, a=a):
            def cells(first, block):
                return ext[a, 0, block, first : first + SEG], ext[a, 1, block, first : first + SEG]

            groups = strip // SEG
            re, im = cells(0, b)
            above = bond(re, im, power_of(re, im), *cells(1, b))
            edge[a, b] = -above[SEG - 1 :]
            batch = min(BATCH, groups)
            for g0 in range(0, groups, batch):
                firsts = [PAD + (g0 + i) * SEG for i in range(batch)]
                here = [cells(first, b) for first in firsts]
                to_right = [
                    [
                        pltpu.roll(jnp.where(lane == 0, after, now), LANES - 1, axis=1)
                        for now, after in zip(here[i], cells(firsts[i], b + 1))
                    ]
                    for i in range(batch)
                ]
                powers = [power_of(*here[i]) for i in range(batch)]
                downs = [bond(*here[i], powers[i], *cells(firsts[i] + 1, b)) for i in range(batch)]
                if g0 + batch == groups:
                    downs[-1] = jnp.where(sub == SEG - 1, 0.0, downs[-1])
                rights = [bond(*here[i], powers[i], *to_right[i]) for i in range(batch)]
                rows = [slice((g0 + i) * SEG, (g0 + i + 1) * SEG) for i in range(batch)]
                from_left = [
                    pltpu.roll(
                        jnp.where(lane == LANES - 1, col_bond[rows[i]], rights[i]), 1, axis=1
                    )
                    for i in range(batch)
                ]
                values = []
                for i in range(batch):
                    from_above = pltpu.roll(
                        jnp.where(sub == SEG - 1, above, downs[i]), 1, axis=0
                    )
                    above = downs[i]
                    values.append(from_above - downs[i] + from_left[i] - rights[i])
                for i in range(batch):
                    col_bond[rows[i]] = rights[i]
                    source[a, b, rows[i]] = values[i]
            return 0

        lax.fori_loop(0, blocks, columns, 0, unroll=2)

    def fold(b, _):
        lanes = pl.ds(pl.multiple_of(b * LANES, LANES), LANES)
        for a in range(angles):
            for t in range(0, steps, 2):
                lower = jnp.concatenate(
                    [source[a, b, pl.ds(t + i, SEG, stride=steps), :] for i in range(2)], 0
                )
                upper = jnp.concatenate(
                    [
                        source[a, blocks - 1 - b, pl.ds(t + i, SEG, stride=steps), :]
                        for i in range(2)
                    ],
                    0,
                )
                upper = reversed_lanes(upper)
                at = a * strip + t * SEG
                for h, values in enumerate((lower + upper, lower - upper)):
                    high, low = split_pair(values)
                    rows_in[h, at : at + 2 * SEG, lanes] = high
                    rows_in[h, count + at : count + at + 2 * SEG, lanes] = low
        edges = [jnp.concatenate([edge[a, i] for a in range(angles)], 0) for i in (b, blocks - 1 - b)]
        fill = jnp.zeros((2 * PAD - angles, LANES), f32)
        lower, upper = (jnp.concatenate([rows, fill], 0) for rows in edges)
        upper = reversed_lanes(upper)
        at = angles * strip
        for h, values in enumerate((lower + upper, lower - upper)):
            high, low = split_pair(values)
            rows_in[h, at : at + 2 * PAD, lanes] = high
            rows_in[h, count + at : count + at + 2 * PAD, lanes] = low
        return 0

    lax.fori_loop(0, half_blocks, fold, 0, unroll=2)

    wide = min(2 * LANES, half)
    sub = lax.broadcasted_iota(jnp.int32, (SEG, wide), 0)
    for h in range(2):

        def transform(c, _, h=h):
            lanes = pl.ds(pl.multiple_of(c * wide, wide), wide)
            spots = pl.ds(pl.multiple_of(h * half + c * wide, wide), wide)
            values = three_pass(rows_in[h], count, table[0, h, :, lanes], table[1, h, :, lanes])
            root = jnp.broadcast_to(scan[0:1, spots], (SEG, wide))
            for a in range(angles):
                terms = [
                    values[a * strip + t * SEG : a * strip + (t + 1) * SEG] for t in range(steps)
                ]
                down = [terms[0]]
                for t in range(1, steps):
                    down.append(terms[t] + root * down[-1])
                up = terms[steps - 1]
                inner[a, (steps - 1) * SEG : steps * SEG, spots] = down[steps - 1]
                for t in range(steps - 2, -1, -1):
                    after = root * up
                    inner[a, t * SEG : (t + 1) * SEG, spots] = down[t] + after
                    up = terms[t] + after
                tail_y, tail_z = down[steps - 1], up
                for i, k in enumerate((1, 2, 4)):
                    factor = scan[i + 1 : i + 2, spots]
                    tail_y = tail_y + jnp.where(
                        sub >= k, factor * pltpu.roll(tail_y, k, axis=0), 0.0
                    )
                    tail_z = tail_z + jnp.where(
                        sub < SEG - k, factor * pltpu.roll(tail_z, SEG - k, axis=0), 0.0
                    )
                above = values[angles * strip + a : angles * strip + a + 1]
                carry_y[a, :, spots] = (
                    jnp.where(sub >= 1, pltpu.roll(tail_y, 1, axis=0), 0.0) + segs[:, spots] * above
                )
                carry_z[a, :, spots] = jnp.where(
                    sub < SEG - 1, pltpu.roll(tail_z, SEG - 1, axis=0), 0.0
                )
                ends[0, a : a + 1, spots] = tail_z[0:1] + scan[5:6, spots] * above
                ends[1, a : a + 1, spots] = tail_y[SEG - 1 : SEG] + scan[6:7, spots] * above
            return 0

        lax.fori_loop(0, half // wide, transform, 0, unroll=4)

    for a in range(angles):
        for b in range(blocks):
            store(a, b).wait()


def run_update(tabs, field, package, halo, scan, segs, tables, pieces, center):
    angles, _, strip, grid = field.shape
    reach = len(pieces) - 1
    blocks = grid // LANES
    half = grid // 2
    return pl.pallas_call(
        functools.partial(update_kernel, reach, center),
        out_shape=[
            jax.ShapeDtypeStruct(field.shape, f32),
            jax.ShapeDtypeStruct((angles, strip, grid), f32),
            jax.ShapeDtypeStruct((angles, SEG, grid), f32),
            jax.ShapeDtypeStruct((angles, SEG, grid), f32),
            jax.ShapeDtypeStruct((2, angles, grid), f32),
        ],
        in_specs=[SMEM_SPEC] * reach
        + [ANY_SPEC]
        + [VMEM_SPEC] * (reach + 6),
        out_specs=[ANY_SPEC] + [VMEM_SPEC] * 4,
        scratch_shapes=[
            pltpu.VMEM((angles, 2, blocks + 1, strip + 2 * PAD, LANES), f32),
            pltpu.VMEM((strip, LANES), f32),
            pltpu.VMEM((angles, blocks, strip, LANES), f32),
            pltpu.VMEM((angles, blocks, 1, LANES), f32),
            pltpu.VMEM((2, 2 * (angles * strip + 2 * PAD), half), bf16),
            pltpu.VMEM((1, LANES), jnp.int32),
            pltpu.SemaphoreType.DMA((angles, blocks)),
            pltpu.SemaphoreType.DMA((angles, blocks)),
        ],
        compiler_params=UPDATE_PARAMS,
        cost_estimate=cost(14),
        name="update",
    )(*tabs, field, package, halo, scan, segs, tables, *pieces)


def phase_kernel(inner, carry_y, carry_z, enter, scan, powers, segs, segs_back, tables, out_hbm, rest, rows_in, table, out, table_sems, out_sems):
    angles, strip, grid = inner.shape
    half = grid // 2
    steps = strip // SEG
    count = angles * strip
    half_blocks = half // LANES
    wide = min(2 * LANES, half)
    chunks = half // wide

    def load_table(c):
        lanes = pl.ds(pl.multiple_of(c * wide, wide), wide)
        return pltpu.make_async_copy(
            tables.at[1, :, :, :, lanes], table.at[:, :, :, lanes], table_sems.at[c]
        )

    def store(c, side):
        start = c * wide if side == 0 else grid - (c + 1) * wide
        lanes = pl.ds(pl.multiple_of(start, wide), wide)
        return pltpu.make_async_copy(
            out.at[:, :, lanes], out_hbm.at[:, :, lanes], out_sems.at[c, side]
        )

    for c in range(chunks):
        load_table(c).start()

    def solve(b, _):
        spots = pl.ds(pl.multiple_of(b * LANES, LANES), LANES)
        scale = scan[4:5, spots]
        for a in range(angles):
            from_y = scale * (carry_y[a, :, spots] + segs[:, spots] * enter[0, a : a + 1, spots])
            from_z = scale * (carry_z[a, :, spots] + segs_back[:, spots] * enter[1, a : a + 1, spots])
            for t in range(steps):
                rest[a, b, pl.ds(t, SEG, stride=steps), :] = (
                    scale * inner[a, t * SEG : (t + 1) * SEG, spots]
                    + powers[t : t + 1, spots] * from_y
                    + powers[steps - 1 - t : steps - t, spots] * from_z
                )
        return 0

    lax.fori_loop(0, 2 * half_blocks, solve, 0, unroll=2)

    def split(b, _):
        lanes = pl.ds(pl.multiple_of(b * LANES, LANES), LANES)
        for h in range(2):
            for a in range(angles):
                high, low = split_pair(rest[a, h * half_blocks + b])
                rows_in[h, a * strip : (a + 1) * strip, lanes] = high
                rows_in[h, count + a * strip : count + (a + 1) * strip, lanes] = low
        return 0

    lax.fori_loop(0, half_blocks, split, 0, unroll=2)

    def back(c, _):
        lanes = pl.ds(pl.multiple_of(c * wide, wide), wide)
        load_table(c).wait()
        even, odd = (
            three_pass(rows_in[h], count, table[0, h, :, lanes], table[1, h, :, lanes])
            for h in range(2)
        )
        mirrored = even - odd
        plain = even + odd
        for a in range(angles):
            out[a, :, lanes] = plain[a * strip : (a + 1) * strip]
            for k in range(wide // LANES):
                spot = pl.ds(
                    pl.multiple_of(grid - (k + 1) * LANES - c * wide, LANES), LANES
                )
                out[a, :, spot] = reversed_lanes(
                    mirrored[a * strip : (a + 1) * strip, k * LANES : (k + 1) * LANES]
                )
        for side in range(2):
            store(c, side).start()
        return 0

    lax.fori_loop(0, chunks, back, 0, unroll=4)
    for c in range(chunks):
        for side in range(2):
            store(c, side).wait()


def run_phase(inner, carry_y, carry_z, enter, scan, powers, segs, segs_back, tables):
    angles, strip, grid = inner.shape
    half = grid // 2
    chunks = half // min(2 * LANES, half)
    return pl.pallas_call(
        phase_kernel,
        out_shape=jax.ShapeDtypeStruct((angles, strip, grid), f32),
        in_specs=[VMEM_SPEC] * 8 + [ANY_SPEC],
        out_specs=ANY_SPEC,
        scratch_shapes=[
            pltpu.VMEM((angles, grid // LANES, strip, LANES), f32),
            pltpu.VMEM((2, 2 * angles * strip, half), bf16),
            pltpu.VMEM(tables.shape[1:], bf16),
            pltpu.VMEM((angles, strip, grid), f32),
            pltpu.SemaphoreType.DMA((chunks,)),
            pltpu.SemaphoreType.DMA((chunks, 2)),
        ],
        compiler_params=PHASE_PARAMS,
        cost_estimate=cost(7),
        name="phase",
    )(inner, carry_y, carry_z, enter, scan, powers, segs, segs_back, tables)


def passed_along(x, by):
    size = lax.axis_size("tile")
    pairs = [(i, i + by) for i in range(size) if 0 <= i + by < size]
    return lax.ppermute(x, "tile", pairs)


def entering_values(ends, strips, closing):
    size = lax.axis_size("tile")
    me = lax.axis_index("tile")
    head, tail = ends[0], ends[1]
    enter_y = jnp.zeros_like(head)
    enter_z = jnp.zeros_like(head)
    row = lambda i: lax.dynamic_slice_in_dim(strips, i, 1, 0)
    width = 1
    while width < size:
        other = lax.ppermute(
            jnp.stack([head, tail]), "tile", [(i, i ^ width) for i in range(size)]
        )
        head_to, tail_to = other[0], other[1]
        second = (me & width) != 0
        before = me & (width - 1)
        span = strips[width : width + 1]
        enter_y = enter_y + jnp.where(second, row(before) * tail_to, 0.0)
        enter_z = enter_z + jnp.where(second, 0.0, row(width - 1 - before) * head_to)
        head, tail = (
            jnp.where(second, head_to + span * head, head + span * head_to),
            jnp.where(second, tail + span * tail_to, tail_to + span * tail),
        )
        width *= 2
    whole = strips[size : size + 1]
    enter_y = enter_y + row(me) * (head + whole * tail) * closing
    enter_z = enter_z + row(size - 1 - me) * (tail + whole * head) * closing
    return jnp.stack([enter_y, enter_z])


def body(object_field, probe, measured, frame_table, frame_count):
    angles, _, strip, grid = object_field.shape
    caps, frame = measured.shape[0], measured.shape[1]
    reach = frame // strip
    center = reach // 2
    halves = cosine_halves(grid)
    forward = jnp.asarray(split_table(np.swapaxes(halves, 1, 2)))
    tables = jnp.asarray(np.stack([split_table(np.swapaxes(halves, 1, 2)), split_table(halves)]))
    scan, powers, segs, segs_back, strips, closing = (
        jnp.asarray(x) for x in decay_tables(grid, strip)
    )

    own_tab = jnp.concatenate(
        [frame_table, jnp.broadcast_to(frame_count[None, :], (caps, 1))], axis=1
    )
    far = [j for j in range(1, reach + 1) if j != center]
    tabs = {0: own_tab}
    for j in far:
        tabs[j] = passed_along(own_tab, j)
    measured_here = passed_along(measured, center)
    package = pack(own_tab, object_field, caps, frame)
    windows = {}
    for j in far:
        window, package = extract(tabs[j], False, object_field, caps, frame, package)
        windows[j] = passed_along(window, center - j)
    arrived = passed_along(package, center)
    at_halo, halo_rows = package_rows(caps, strip, frame, angles, grid)
    halo = slice(at_halo, at_halo + 3 * halo_rows)
    top = arrived[halo] if center == 1 else passed_along(package[halo], 1)
    windows[center] = extract(arrived, True, object_field, caps, frame)
    pieces = run_frames(arrived, measured_here, probe, [windows[j] for j in range(1, reach + 1)], center)
    pieces = [
        piece if j == center else passed_along(piece, j - center) for j, piece in enumerate(pieces)
    ]
    updated, inner, carry_y, carry_z, ends = run_update(
        [tabs[j] for j in range(reach + 1) if j != center],
        object_field,
        arrived,
        top,
        scan,
        segs,
        forward,
        pieces,
        center,
    )
    enter = entering_values(ends, strips, closing)
    phase_map = run_phase(
        inner, carry_y, carry_z, enter, scan, powers, segs, segs_back, tables
    )
    return (updated, phase_map)


def solution(mesh):
    return jax.shard_map(
        body,
        mesh=mesh,
        in_specs=(
            P("group", None, "tile", None),
            P(),
            P(("group", "tile"), None, None),
            P(("group", "tile"), None),
            P(("group", "tile")),
        ),
        out_specs=(P("group", None, "tile", None), P("group", "tile", None)),
        check_vma=False,
    )
```

```python
import functools
import math

import jax
import jax.numpy as jnp
import ml_dtypes
import numpy as np
from jax import lax
from jax.experimental import pallas as pl
from jax.experimental.pallas import tpu as pltpu
from jax.sharding import PartitionSpec as P

magnitude_floor = 0.5
soften_term = 0.5
screen_term = 0.0001
epsilon_term = 1e-06
LANES = 128
SEG = 8
PAD = 8
f32 = jnp.float32
bf16 = jnp.bfloat16
VMEM_SPEC = pl.BlockSpec(memory_space=pltpu.VMEM)
SMEM_SPEC = pl.BlockSpec(memory_space=pltpu.SMEM)
ANY_SPEC = pl.BlockSpec(memory_space=pl.ANY)
PARAMS = pltpu.CompilerParams(vmem_limit_bytes=26 * 1024 * 1024)
UPDATE_PARAMS = pltpu.CompilerParams(vmem_limit_bytes=32 * 1024 * 1024)
PHASE_PARAMS = pltpu.CompilerParams(vmem_limit_bytes=46 * 1024 * 1024)
DIGIT = 64
CODE_ROWS = 16
FIELDS = 4
BATCH = 16


def cost(micros):
    return pl.CostEstimate(flops=0, bytes_accessed=int(micros * 3.0e6), transcendentals=0)


def split_table(table):
    high = table.astype(ml_dtypes.bfloat16)
    low = (table - high.astype(np.float64)).astype(ml_dtypes.bfloat16)
    return np.stack([high, low])


def fourier_blocks(side):
    index = np.arange(side)
    phase = (index[:, None] * index[None, :] % side) * (-2.0 * math.pi / side)
    cos_part = np.cos(phase) / math.sqrt(side)
    sin_part = np.sin(phase) / math.sqrt(side)
    left = np.block([[cos_part, -sin_part], [sin_part, cos_part]])
    right = np.block([[cos_part, sin_part], [-sin_part, cos_part]])
    return left.astype(ml_dtypes.bfloat16), right.astype(ml_dtypes.bfloat16)


def cosine_halves(grid):
    half = grid // 2
    freqs = np.arange(grid)
    pixels = np.arange(half)
    phase = (2 * pixels[None, :] + 1) * freqs[:, None] % (4 * grid)
    scale = np.where(freqs == 0, math.sqrt(1.0 / grid), math.sqrt(2.0 / grid))
    table = scale[:, None] * np.cos(phase * (math.pi / (2 * grid)))
    return np.stack([table[0::2], table[1::2]])


def decay_tables(grid, strip):
    freqs = np.concatenate([np.arange(0, grid, 2), np.arange(1, grid, 2)])
    mu = screen_term + 4.0 * np.sin(freqs * (math.pi / (2 * grid))) ** 2
    root = 1.0 + mu / 2 - np.sqrt(mu + mu * mu / 4)
    log_root = np.log(root)
    steps = strip // SEG
    devices = grid // strip

    def power(exponents):
        return np.exp(np.maximum(log_root[None, :] * np.asarray(exponents)[:, None], -80.0)) * (
            log_root[None, :] * np.asarray(exponents)[:, None] > -80.0
        )

    scan = np.concatenate(
        [
            power([1, steps, 2 * steps, 4 * steps]),
            (2 * root / (1 - root * root))[None],
            (1 / root)[None],
            power([strip]),
        ]
    )
    inner = power(np.arange(1, steps + 1))
    segs = power(steps * np.arange(SEG))
    strips = power(strip * np.arange(devices + 1))
    closing = 1.0 / (1.0 - power([2 * grid]))
    as32 = lambda x: x.astype(np.float32)
    return as32(scan), as32(inner), as32(segs), as32(segs[::-1]), as32(strips), as32(closing)


def clip(value, top):
    return jnp.minimum(jnp.maximum(value, 0), top)


def window_copies(tab, field, raw, sems):
    caps, wide = raw.shape[0], raw.shape[3]
    frame = wide - LANES
    angles, grid = field.shape[0], field.shape[3]
    copies = []
    for slot in range(caps):
        column = clip(tab(slot, 1), grid - frame)
        angle = clip(tab(slot, 2), angles - 1)
        block = jnp.minimum(column // LANES, (grid - wide) // LANES)
        start = pl.multiple_of(block * LANES, LANES)
        copy = pltpu.make_async_copy(
            field.at[angle, :, :, pl.ds(start, wide)], raw.at[slot], sems.at[slot]
        )
        copy.start()
        copies.append((copy, lax.rem(wide - (column - block * LANES), wide)))
    return copies


def window_values(copies, raw, slot, part):
    wide = raw.shape[3]
    return pltpu.roll(raw[slot, part], copies[slot][1], axis=1)[:, : wide - LANES].astype(bf16)


def decoded(package, ints):
    rows = package.shape[0]
    digits = package[rows - CODE_ROWS :, :LANES].astype(f32)
    ints[...] = (digits[0:1] * DIGIT + digits[1:2]).astype(jnp.int32)
    return lambda slot, i: ints[0, slot * FIELDS + i]


def plain(tab):
    return lambda slot, i: tab[slot, i]


def package_rows(caps, strip, frame, angles, grid):
    windows = caps * 2 * strip
    halo = angles * 2 * grid // frame
    return windows, halo


def pack_kernel(caps, tab, field, out, raw, last_rows, halo_buf, sems, row_sem):
    frame = out.shape[1]
    angles, _, strip, grid = field.shape
    at_halo, halo_rows = package_rows(caps, strip, frame, angles, grid)
    copies = window_copies(plain(tab), field, raw, sems)
    row_copy = pltpu.make_async_copy(
        field.at[:, :, pl.ds(strip - PAD, PAD), :], last_rows, row_sem.at[0]
    )
    row_copy.start()
    place = lax.broadcasted_iota(jnp.int32, (CODE_ROWS, frame), 1)
    row = lax.broadcasted_iota(jnp.int32, (CODE_ROWS, frame), 0)
    high = jnp.zeros((CODE_ROWS, frame), jnp.int32)
    low = jnp.zeros((CODE_ROWS, frame), jnp.int32)
    for slot in range(caps):
        for i in range(FIELDS):
            here = place == slot * FIELDS + i
            high = jnp.where(here, tab[slot, i] // DIGIT, high)
            low = jnp.where(here, lax.rem(tab[slot, i], DIGIT), low)
    code = jnp.where(row == 0, high, jnp.where(row == 1, low, 0))
    out[out.shape[0] - CODE_ROWS :] = code.astype(f32).astype(bf16)
    row_copy.wait()
    per_row = grid // frame
    for a in range(angles):
        for part in range(2):
            for k in range(per_row):
                i = (a * 2 + part) * per_row + k
                halo_buf[i : i + 1] = last_rows[a, part, PAD - 1 :, k * frame : (k + 1) * frame]
    left_over = halo_buf[...]
    for i in range(3):
        digit = left_over.astype(bf16)
        out[at_halo + i * halo_rows : at_halo + (i + 1) * halo_rows] = digit
        left_over = left_over - digit.astype(f32)
    for slot in range(caps):
        copies[slot][0].wait()
        for part in range(2):
            at = (slot * 2 + part) * strip
            out[at : at + strip] = window_values(copies, raw, slot, part)


def pack(tab, field, caps, frame):
    angles, _, strip, grid = field.shape
    at_halo, halo_rows = package_rows(caps, strip, frame, angles, grid)
    return pl.pallas_call(
        functools.partial(pack_kernel, caps),
        out_shape=jax.ShapeDtypeStruct((at_halo + 3 * halo_rows + CODE_ROWS, frame), bf16),
        in_specs=[SMEM_SPEC, ANY_SPEC],
        out_specs=VMEM_SPEC,
        scratch_shapes=[
            pltpu.VMEM((caps, 2, strip, frame + LANES), f32),
            pltpu.VMEM((angles, 2, PAD, grid), f32),
            pltpu.VMEM((halo_rows, frame), f32),
            pltpu.SemaphoreType.DMA((caps,)),
            pltpu.SemaphoreType.DMA((1,)),
        ],
        compiler_params=PARAMS,
        cost_estimate=cost(6),
        name="pack",
    )(tab, field)


def extract_kernel(coded, tab, field, *rest):
    raw, ints, sems = rest[-3:]
    out = rest[0] if coded else rest[1]
    read = decoded(tab, ints) if coded else plain(tab)
    copies = window_copies(read, field, raw, sems)
    for slot in range(out.shape[0]):
        copies[slot][0].wait()
        for part in range(2):
            out[slot, part] = window_values(copies, raw, slot, part)


def extract(tab, coded, field, caps, frame, package=None):
    angles, _, strip, grid = field.shape
    window = jax.ShapeDtypeStruct((caps, 2, strip, frame), bf16)
    through = [] if coded else [package]
    out = pl.pallas_call(
        functools.partial(extract_kernel, coded),
        out_shape=[window] + [jax.ShapeDtypeStruct(x.shape, x.dtype) for x in through],
        in_specs=[VMEM_SPEC if coded else SMEM_SPEC, ANY_SPEC] + [ANY_SPEC] * len(through),
        out_specs=[VMEM_SPEC] + [ANY_SPEC] * len(through),
        input_output_aliases={2: 1} if through else {},
        scratch_shapes=[
            pltpu.VMEM((caps, 2, strip, frame + LANES), f32),
            pltpu.VMEM((1, LANES), jnp.int32),
            pltpu.SemaphoreType.DMA((caps,)),
        ],
        compiler_params=PARAMS,
        cost_estimate=cost(2),
        name="extract",
    )(tab, field, *through)
    return out[0] if coded else out


def frame_kernel(reach, package, measured, probe, left, right, *rest):
    windows = rest[:reach]
    pieces = rest[reach : 2 * reach + 1]
    window_buf, update_buf, ints = rest[2 * reach + 1 :]
    caps, _, strip, frame = windows[0].shape
    read = decoded(package, ints)
    blocks = frame // LANES
    count = read(0, 3)
    probe_re, probe_im = probe[0], probe[1]
    peak = jnp.max(probe_re * probe_re + probe_im * probe_im) + epsilon_term
    for slot in range(caps):
        update_buf[...] = jnp.zeros_like(update_buf)

        @pl.when(slot < count)
        def _():
            offset = clip(read(slot, 0), strip - 1)
            for j in range(reach + 1):
                for part in range(2):
                    for k in range(blocks):
                        lanes = slice(k * LANES, (k + 1) * LANES)
                        at = (slot * 2 + part) * strip
                        values = (
                            windows[j - 1][slot, part, :, lanes]
                            if j
                            else package[at : at + strip, lanes]
                        )
                        window_buf[part, k, j * strip : (j + 1) * strip] = values.astype(f32)
            obj_re, obj_im = (
                jnp.concatenate(
                    [window_buf[part, k, pl.ds(offset, frame), :] for k in range(blocks)], axis=1
                )
                for part in range(2)
            )
            wave = jnp.concatenate(
                [
                    (probe_re * obj_re - probe_im * obj_im).astype(bf16),
                    (probe_re * obj_im + probe_im * obj_re).astype(bf16),
                ],
                axis=0,
            )

            def both(first, second, rows):
                first_half = jnp.dot(first, rows, preferred_element_type=f32).astype(bf16)
                beside = jnp.concatenate([first_half[:frame], first_half[frame:]], axis=1)
                return jnp.dot(beside, second, preferred_element_type=f32)

            spectrum = both(left[...], right[...], wave)
            spec_re, spec_im = spectrum[:, :frame], spectrum[:, frame:]
            power = spec_re * spec_re + spec_im * spec_im
            factor = (
                measured[slot].astype(f32)
                * lax.rsqrt(jnp.maximum(power, magnitude_floor**2)) - 1.0
            )
            change = jnp.concatenate(
                [(spec_re * factor).astype(bf16), (spec_im * factor).astype(bf16)], axis=0
            )
            correction = both(right[...], left[...], change)
            corr_re, corr_im = correction[:, :frame], correction[:, frame:]
            update = (
                (probe_re * corr_re + probe_im * corr_im) / peak,
                (probe_re * corr_im - probe_im * corr_re) / peak,
            )
            for part in range(2):
                for k in range(blocks):
                    update_buf[part, k, pl.ds(2 * PAD + offset, frame), :] = update[part][
                        :, k * LANES : (k + 1) * LANES
                    ]

        for part in range(2):
            for k in range(blocks):
                lanes = slice(k * LANES, (k + 1) * LANES)
                for j in range(reach + 1):
                    rim = PAD if j else 0
                    first = j * strip + 2 * PAD
                    pieces[j][slot, part, :, lanes] = update_buf[
                        part, k, first - rim : first + strip + rim
                    ].astype(pieces[j].dtype)


def run_frames(package, measured, probe, windows, center):
    reach = len(windows)
    caps, _, strip, frame = windows[0].shape
    left, right = fourier_blocks(frame)
    rows = (reach + 1) * strip
    piece = lambda j: jax.ShapeDtypeStruct(
        (caps, 2, strip + (2 * PAD if j else 0), frame), f32 if j == center else bf16
    )
    return pl.pallas_call(
        functools.partial(frame_kernel, reach),
        out_shape=[piece(j) for j in range(reach + 1)],
        in_specs=[VMEM_SPEC] * (5 + reach),
        out_specs=[VMEM_SPEC] * (reach + 1),
        scratch_shapes=[
            pltpu.VMEM((2, frame // LANES, rows, LANES), f32),
            pltpu.VMEM((2, frame // LANES, rows + 4 * PAD, LANES), f32),
            pltpu.VMEM((1, LANES), jnp.int32),
        ],
        compiler_params=PARAMS,
        cost_estimate=cost(5),
        name="frames",
    )(package, measured, probe, jnp.asarray(left), jnp.asarray(right), *windows)


def reversed_lanes(values):
    index = LANES - 1 - lax.broadcasted_iota(jnp.int32, values.shape, 1)
    return jnp.take_along_axis(values, index, axis=1)


def split_pair(values):
    high = values.astype(bf16)
    return high, (values - high.astype(f32)).astype(bf16)


def three_pass(rows, count, high, low):
    both = jnp.dot(rows, high, preferred_element_type=f32)
    return both[:count] + both[count:] + jnp.dot(rows[:count], low, preferred_element_type=f32)


def update_kernel(reach, center, *refs):
    tabs = refs[:reach]
    field, package, halo, scan, segs, table, *rest = refs[reach:]
    tabs = tabs[:center] + (None,) + tabs[center:]
    pieces = rest[: reach + 1]
    updated, inner, carry_y, carry_z, ends = rest[reach + 1 : reach + 6]
    ext, col_bond, source, edge, rows_in, ints, load_sems, store_sems = rest[reach + 6 :]
    angles, _, strip, grid = field.shape
    blocks = grid // LANES
    half_blocks = blocks // 2
    half = grid // 2
    steps = strip // SEG
    count = angles * strip + 2 * PAD
    caps = pieces[0].shape[0]
    frame = pieces[0].shape[3]
    frame_blocks = frame // LANES

    def load(a, b):
        start = b * LANES
        return pltpu.make_async_copy(
            field.at[a, :, :, pl.ds(start, LANES)],
            ext.at[a, :, b, pl.ds(PAD, strip), :],
            load_sems.at[a, b],
        )

    def store(a, b):
        start = b * LANES
        return pltpu.make_async_copy(
            ext.at[a, :, b, pl.ds(PAD, strip), :],
            updated.at[a, :, :, pl.ds(start, LANES)],
            store_sems.at[a, b],
        )

    for a in range(angles):
        for b in range(blocks):
            load(a, b).start()
    halo_rows = halo.shape[0] // 3
    top = sum(halo[i * halo_rows : (i + 1) * halo_rows].astype(f32) for i in range(3))
    per_row = grid // frame
    read = decoded(package, ints)
    for a in range(angles):
        for part in range(2):
            for b in range(blocks):
                row = (a * 2 + part) * per_row + b // frame_blocks
                lanes = slice(b % frame_blocks * LANES, (b % frame_blocks + 1) * LANES)
                ext[a, part, b, PAD - 1 : PAD, :] = top[row : row + 1, lanes]
            ext[a, part, blocks] = jnp.zeros((strip + 2 * PAD, LANES), f32)
    for a in range(angles):
        for b in range(blocks):
            load(a, b).wait()

    def add_piece(piece, tab, slot):
        @pl.when(slot < tab(0, 3))
        def _():
            column = clip(tab(slot, 1), grid - frame)
            angle = clip(tab(slot, 2), angles - 1)
            block = jnp.minimum(column // LANES, blocks - frame_blocks - 1)
            shift = column - block * LANES
            for part in range(2):
                values = piece[slot, part].astype(f32)
                rows = values.shape[0]
                first = PAD + (strip - rows) // 2
                values = jnp.concatenate([values, jnp.zeros((rows, LANES), f32)], axis=1)
                values = pltpu.roll(values, shift, axis=1)
                for k in range(frame_blocks + 1):
                    spot = ext.at[angle, part, block + k, first : first + rows]
                    spot[...] += values[:, k * LANES : (k + 1) * LANES]

    for slot in range(caps):
        for j in range(reach + 1):
            add_piece(pieces[j], read if j == center else plain(tabs[j]), slot)

    for a in range(angles):
        for b in range(blocks):
            store(a, b).start()

    lane = lax.broadcasted_iota(jnp.int32, (SEG, LANES), 1)
    sub = lax.broadcasted_iota(jnp.int32, (SEG, LANES), 0)

    def power_of(re, im):
        return re * re + (im * im + 0.5 * soften_term)

    def bond(re, im, power, re_to, im_to):
        return (re * im_to - im * re_to) * pl.reciprocal(
            power + power_of(re_to, im_to), approx=True
        )

    for a in range(angles):
        col_bond[...] = jnp.zeros_like(col_bond)

        def columns(b, _, a=a):
            def cells(first, block):
                return ext[a, 0, block, first : first + SEG], ext[a, 1, block, first : first + SEG]

            groups = strip // SEG
            re, im = cells(0, b)
            above = bond(re, im, power_of(re, im), *cells(1, b))
            edge[a, b] = -above[SEG - 1 :]
            batch = min(BATCH, groups)
            for g0 in range(0, groups, batch):
                firsts = [PAD + (g0 + i) * SEG for i in range(batch)]
                here = [cells(first, b) for first in firsts]
                to_right = [
                    [
                        pltpu.roll(jnp.where(lane == 0, after, now), LANES - 1, axis=1)
                        for now, after in zip(here[i], cells(firsts[i], b + 1))
                    ]
                    for i in range(batch)
                ]
                powers = [power_of(*here[i]) for i in range(batch)]
                downs = [bond(*here[i], powers[i], *cells(firsts[i] + 1, b)) for i in range(batch)]
                if g0 + batch == groups:
                    downs[-1] = jnp.where(sub == SEG - 1, 0.0, downs[-1])
                rights = [bond(*here[i], powers[i], *to_right[i]) for i in range(batch)]
                rows = [slice((g0 + i) * SEG, (g0 + i + 1) * SEG) for i in range(batch)]
                from_left = [
                    pltpu.roll(
                        jnp.where(lane == LANES - 1, col_bond[rows[i]], rights[i]), 1, axis=1
                    )
                    for i in range(batch)
                ]
                values = []
                for i in range(batch):
                    from_above = pltpu.roll(
                        jnp.where(sub == SEG - 1, above, downs[i]), 1, axis=0
                    )
                    above = downs[i]
                    values.append(from_above - downs[i] + from_left[i] - rights[i])
                for i in range(batch):
                    col_bond[rows[i]] = rights[i]
                    source[a, b, rows[i]] = values[i]
            return 0

        lax.fori_loop(0, blocks, columns, 0, unroll=2)

    def fold(b, _):
        lanes = pl.ds(pl.multiple_of(b * LANES, LANES), LANES)
        for a in range(angles):
            for t in range(0, steps, 2):
                lower = jnp.concatenate(
                    [source[a, b, pl.ds(t + i, SEG, stride=steps), :] for i in range(2)], 0
                )
                upper = jnp.concatenate(
                    [
                        source[a, blocks - 1 - b, pl.ds(t + i, SEG, stride=steps), :]
                        for i in range(2)
                    ],
                    0,
                )
                upper = reversed_lanes(upper)
                at = a * strip + t * SEG
                for h, values in enumerate((lower + upper, lower - upper)):
                    high, low = split_pair(values)
                    rows_in[h, at : at + 2 * SEG, lanes] = high
                    rows_in[h, count + at : count + at + 2 * SEG, lanes] = low
        edges = [jnp.concatenate([edge[a, i] for a in range(angles)], 0) for i in (b, blocks - 1 - b)]
        fill = jnp.zeros((2 * PAD - angles, LANES), f32)
        lower, upper = (jnp.concatenate([rows, fill], 0) for rows in edges)
        upper = reversed_lanes(upper)
        at = angles * strip
        for h, values in enumerate((lower + upper, lower - upper)):
            high, low = split_pair(values)
            rows_in[h, at : at + 2 * PAD, lanes] = high
            rows_in[h, count + at : count + at + 2 * PAD, lanes] = low
        return 0

    lax.fori_loop(0, half_blocks, fold, 0, unroll=2)

    wide = min(2 * LANES, half)
    sub = lax.broadcasted_iota(jnp.int32, (SEG, wide), 0)
    for h in range(2):

        def transform(c, _, h=h):
            lanes = pl.ds(pl.multiple_of(c * wide, wide), wide)
            spots = pl.ds(pl.multiple_of(h * half + c * wide, wide), wide)
            values = three_pass(rows_in[h], count, table[0, h, :, lanes], table[1, h, :, lanes])
            root = jnp.broadcast_to(scan[0:1, spots], (SEG, wide))
            for a in range(angles):
                terms = [
                    values[a * strip + t * SEG : a * strip + (t + 1) * SEG] for t in range(steps)
                ]
                down = [terms[0]]
                for t in range(1, steps):
                    down.append(terms[t] + root * down[-1])
                up = terms[steps - 1]
                inner[a, (steps - 1) * SEG : steps * SEG, spots] = down[steps - 1]
                for t in range(steps - 2, -1, -1):
                    after = root * up
                    inner[a, t * SEG : (t + 1) * SEG, spots] = down[t] + after
                    up = terms[t] + after
                tail_y, tail_z = down[steps - 1], up
                for i, k in enumerate((1, 2, 4)):
                    factor = scan[i + 1 : i + 2, spots]
                    tail_y = tail_y + jnp.where(
                        sub >= k, factor * pltpu.roll(tail_y, k, axis=0), 0.0
                    )
                    tail_z = tail_z + jnp.where(
                        sub < SEG - k, factor * pltpu.roll(tail_z, SEG - k, axis=0), 0.0
                    )
                above = values[angles * strip + a : angles * strip + a + 1]
                carry_y[a, :, spots] = (
                    jnp.where(sub >= 1, pltpu.roll(tail_y, 1, axis=0), 0.0) + segs[:, spots] * above
                )
                carry_z[a, :, spots] = jnp.where(
                    sub < SEG - 1, pltpu.roll(tail_z, SEG - 1, axis=0), 0.0
                )
                ends[0, a : a + 1, spots] = tail_z[0:1] + scan[5:6, spots] * above
                ends[1, a : a + 1, spots] = tail_y[SEG - 1 : SEG] + scan[6:7, spots] * above
            return 0

        lax.fori_loop(0, half // wide, transform, 0, unroll=4)

    for a in range(angles):
        for b in range(blocks):
            store(a, b).wait()


def run_update(tabs, field, package, halo, scan, segs, tables, pieces, center):
    angles, _, strip, grid = field.shape
    reach = len(pieces) - 1
    blocks = grid // LANES
    half = grid // 2
    return pl.pallas_call(
        functools.partial(update_kernel, reach, center),
        out_shape=[
            jax.ShapeDtypeStruct(field.shape, f32),
            jax.ShapeDtypeStruct((angles, strip, grid), f32),
            jax.ShapeDtypeStruct((angles, SEG, grid), f32),
            jax.ShapeDtypeStruct((angles, SEG, grid), f32),
            jax.ShapeDtypeStruct((2, angles, grid), f32),
        ],
        in_specs=[SMEM_SPEC] * reach
        + [ANY_SPEC]
        + [VMEM_SPEC] * (reach + 6),
        out_specs=[ANY_SPEC] + [VMEM_SPEC] * 4,
        scratch_shapes=[
            pltpu.VMEM((angles, 2, blocks + 1, strip + 2 * PAD, LANES), f32),
            pltpu.VMEM((strip, LANES), f32),
            pltpu.VMEM((angles, blocks, strip, LANES), f32),
            pltpu.VMEM((angles, blocks, 1, LANES), f32),
            pltpu.VMEM((2, 2 * (angles * strip + 2 * PAD), half), bf16),
            pltpu.VMEM((1, LANES), jnp.int32),
            pltpu.SemaphoreType.DMA((angles, blocks)),
            pltpu.SemaphoreType.DMA((angles, blocks)),
        ],
        compiler_params=UPDATE_PARAMS,
        cost_estimate=cost(14),
        name="update",
    )(*tabs, field, package, halo, scan, segs, tables, *pieces)


def phase_kernel(inner, carry_y, carry_z, enter, scan, powers, segs, segs_back, tables, out_hbm, rest, rows_in, table, out, table_sems, out_sems):
    angles, strip, grid = inner.shape
    half = grid // 2
    steps = strip // SEG
    count = angles * strip
    half_blocks = half // LANES
    wide = min(2 * LANES, half)
    chunks = half // wide

    def load_table(c):
        lanes = pl.ds(pl.multiple_of(c * wide, wide), wide)
        return pltpu.make_async_copy(
            tables.at[1, :, :, :, lanes], table.at[:, :, :, lanes], table_sems.at[c]
        )

    def store(c, side):
        start = c * wide if side == 0 else grid - (c + 1) * wide
        lanes = pl.ds(pl.multiple_of(start, wide), wide)
        return pltpu.make_async_copy(
            out.at[:, :, lanes], out_hbm.at[:, :, lanes], out_sems.at[c, side]
        )

    for c in range(chunks):
        load_table(c).start()

    def solve(b, _):
        spots = pl.ds(pl.multiple_of(b * LANES, LANES), LANES)
        scale = scan[4:5, spots]
        for a in range(angles):
            from_y = scale * (carry_y[a, :, spots] + segs[:, spots] * enter[0, a : a + 1, spots])
            from_z = scale * (carry_z[a, :, spots] + segs_back[:, spots] * enter[1, a : a + 1, spots])
            for t in range(steps):
                rest[a, b, pl.ds(t, SEG, stride=steps), :] = (
                    scale * inner[a, t * SEG : (t + 1) * SEG, spots]
                    + powers[t : t + 1, spots] * from_y
                    + powers[steps - 1 - t : steps - t, spots] * from_z
                )
        return 0

    lax.fori_loop(0, 2 * half_blocks, solve, 0, unroll=2)

    def split(b, _):
        lanes = pl.ds(pl.multiple_of(b * LANES, LANES), LANES)
        for h in range(2):
            for a in range(angles):
                high, low = split_pair(rest[a, h * half_blocks + b])
                rows_in[h, a * strip : (a + 1) * strip, lanes] = high
                rows_in[h, count + a * strip : count + (a + 1) * strip, lanes] = low
        return 0

    lax.fori_loop(0, half_blocks, split, 0, unroll=2)

    def back(c, _):
        lanes = pl.ds(pl.multiple_of(c * wide, wide), wide)
        load_table(c).wait()
        even, odd = (
            three_pass(rows_in[h], count, table[0, h, :, lanes], table[1, h, :, lanes])
            for h in range(2)
        )
        mirrored = even - odd
        plain = even + odd
        for a in range(angles):
            out[a, :, lanes] = plain[a * strip : (a + 1) * strip]
            for k in range(wide // LANES):
                spot = pl.ds(
                    pl.multiple_of(grid - (k + 1) * LANES - c * wide, LANES), LANES
                )
                out[a, :, spot] = reversed_lanes(
                    mirrored[a * strip : (a + 1) * strip, k * LANES : (k + 1) * LANES]
                )
        for side in range(2):
            store(c, side).start()
        return 0

    lax.fori_loop(0, chunks, back, 0, unroll=4)
    for c in range(chunks):
        for side in range(2):
            store(c, side).wait()


def run_phase(inner, carry_y, carry_z, enter, scan, powers, segs, segs_back, tables):
    angles, strip, grid = inner.shape
    half = grid // 2
    chunks = half // min(2 * LANES, half)
    return pl.pallas_call(
        phase_kernel,
        out_shape=jax.ShapeDtypeStruct((angles, strip, grid), f32),
        in_specs=[VMEM_SPEC] * 8 + [ANY_SPEC],
        out_specs=ANY_SPEC,
        scratch_shapes=[
            pltpu.VMEM((angles, grid // LANES, strip, LANES), f32),
            pltpu.VMEM((2, 2 * angles * strip, half), bf16),
            pltpu.VMEM(tables.shape[1:], bf16),
            pltpu.VMEM((angles, strip, grid), f32),
            pltpu.SemaphoreType.DMA((chunks,)),
            pltpu.SemaphoreType.DMA((chunks, 2)),
        ],
        compiler_params=PHASE_PARAMS,
        cost_estimate=cost(7),
        name="phase",
    )(inner, carry_y, carry_z, enter, scan, powers, segs, segs_back, tables)


def passed_along(x, by):
    size = lax.axis_size("tile")
    pairs = [(i, i + by) for i in range(size) if 0 <= i + by < size]
    return lax.ppermute(x, "tile", pairs)


def entering_values(ends, strips, closing):
    size = lax.axis_size("tile")
    me = lax.axis_index("tile")
    head, tail = ends[0], ends[1]
    enter_y = jnp.zeros_like(head)
    enter_z = jnp.zeros_like(head)
    row = lambda i: lax.dynamic_slice_in_dim(strips, i, 1, 0)
    width = 1
    while width < size:
        other = lax.ppermute(
            jnp.stack([head, tail]), "tile", [(i, i ^ width) for i in range(size)]
        )
        head_to, tail_to = other[0], other[1]
        second = (me & width) != 0
        before = me & (width - 1)
        span = strips[width : width + 1]
        enter_y = enter_y + jnp.where(second, row(before) * tail_to, 0.0)
        enter_z = enter_z + jnp.where(second, 0.0, row(width - 1 - before) * head_to)
        head, tail = (
            jnp.where(second, head_to + span * head, head + span * head_to),
            jnp.where(second, tail + span * tail_to, tail_to + span * tail),
        )
        width *= 2
    whole = strips[size : size + 1]
    enter_y = enter_y + row(me) * (head + whole * tail) * closing
    enter_z = enter_z + row(size - 1 - me) * (tail + whole * head) * closing
    return jnp.stack([enter_y, enter_z])


def body(object_field, probe, measured, frame_table, frame_count):
    angles, _, strip, grid = object_field.shape
    caps, frame = measured.shape[0], measured.shape[1]
    reach = frame // strip
    center = reach // 2
    halves = cosine_halves(grid)
    forward = jnp.asarray(split_table(np.swapaxes(halves, 1, 2)))
    tables = jnp.asarray(np.stack([split_table(np.swapaxes(halves, 1, 2)), split_table(halves)]))
    scan, powers, segs, segs_back, strips, closing = (
        jnp.asarray(x) for x in decay_tables(grid, strip)
    )

    own_tab = jnp.concatenate(
        [frame_table, jnp.broadcast_to(frame_count[None, :], (caps, 1))], axis=1
    )
    far = [j for j in range(1, reach + 1) if j != center]
    tabs = {0: own_tab}
    for j in far:
        tabs[j] = passed_along(own_tab, j)
    measured_here = passed_along(measured, center)
    package = pack(own_tab, object_field, caps, frame)
    windows = {}
    for j in far:
        window, package = extract(tabs[j], False, object_field, caps, frame, package)
        windows[j] = passed_along(window, center - j)
    arrived = passed_along(package, center)
    at_halo, halo_rows = package_rows(caps, strip, frame, angles, grid)
    halo = slice(at_halo, at_halo + 3 * halo_rows)
    top = arrived[halo] if center == 1 else passed_along(package[halo], 1)
    windows[center] = extract(arrived, True, object_field, caps, frame)
    pieces = run_frames(arrived, measured_here, probe, [windows[j] for j in range(1, reach + 1)], center)
    pieces = [
        piece if j == center else passed_along(piece, j - center) for j, piece in enumerate(pieces)
    ]
    updated, inner, carry_y, carry_z, ends = run_update(
        [tabs[j] for j in range(reach + 1) if j != center],
        object_field,
        arrived,
        top,
        scan,
        segs,
        forward,
        pieces,
        center,
    )
    enter = entering_values(ends, strips, closing)
    phase_map = run_phase(
        inner, carry_y, carry_z, enter, scan, powers, segs, segs_back, tables
    )
    return (updated, phase_map)


def solution(mesh):
    return jax.shard_map(
        body,
        mesh=mesh,
        in_specs=(
            P("group", None, "tile", None),
            P(),
            P(("group", "tile"), None, None),
            P(("group", "tile"), None),
            P(("group", "tile")),
        ),
        out_specs=(P("group", None, "tile", None), P("group", "tile", None)),
        check_vma=False,
    )
```

```python
import functools
import math

import jax
import jax.numpy as jnp
import ml_dtypes
import numpy as np
from jax import lax
from jax.experimental import pallas as pl
from jax.experimental.pallas import tpu as pltpu
from jax.sharding import PartitionSpec as P

magnitude_floor = 0.5
soften_term = 0.5
screen_term = 0.0001
epsilon_term = 1e-06
LANES = 128
SEG = 8
PAD = 8
f32 = jnp.float32
bf16 = jnp.bfloat16
VMEM_SPEC = pl.BlockSpec(memory_space=pltpu.VMEM)
SMEM_SPEC = pl.BlockSpec(memory_space=pltpu.SMEM)
ANY_SPEC = pl.BlockSpec(memory_space=pl.ANY)
PARAMS = pltpu.CompilerParams(vmem_limit_bytes=26 * 1024 * 1024)
UPDATE_PARAMS = pltpu.CompilerParams(vmem_limit_bytes=32 * 1024 * 1024)
PHASE_PARAMS = pltpu.CompilerParams(vmem_limit_bytes=46 * 1024 * 1024)
DIGIT = 64
CODE_ROWS = 16
FIELDS = 4
BATCH = 16


def cost(micros):
    return pl.CostEstimate(flops=0, bytes_accessed=int(micros * 3.0e6), transcendentals=0)


def split_table(table):
    high = table.astype(ml_dtypes.bfloat16)
    low = (table - high.astype(np.float64)).astype(ml_dtypes.bfloat16)
    return np.stack([high, low])


def fourier_blocks(side):
    index = np.arange(side)
    phase = (index[:, None] * index[None, :] % side) * (-2.0 * math.pi / side)
    cos_part = np.cos(phase) / math.sqrt(side)
    sin_part = np.sin(phase) / math.sqrt(side)
    left = np.block([[cos_part, -sin_part], [sin_part, cos_part]])
    right = np.block([[cos_part, sin_part], [-sin_part, cos_part]])
    return left.astype(ml_dtypes.bfloat16), right.astype(ml_dtypes.bfloat16)


def cosine_halves(grid):
    half = grid // 2
    freqs = np.arange(grid)
    pixels = np.arange(half)
    phase = (2 * pixels[None, :] + 1) * freqs[:, None] % (4 * grid)
    scale = np.where(freqs == 0, math.sqrt(1.0 / grid), math.sqrt(2.0 / grid))
    table = scale[:, None] * np.cos(phase * (math.pi / (2 * grid)))
    return np.stack([table[0::2], table[1::2]])


def decay_tables(grid, strip):
    freqs = np.concatenate([np.arange(0, grid, 2), np.arange(1, grid, 2)])
    mu = screen_term + 4.0 * np.sin(freqs * (math.pi / (2 * grid))) ** 2
    root = 1.0 + mu / 2 - np.sqrt(mu + mu * mu / 4)
    log_root = np.log(root)
    steps = strip // SEG
    devices = grid // strip

    def power(exponents):
        return np.exp(np.maximum(log_root[None, :] * np.asarray(exponents)[:, None], -80.0)) * (
            log_root[None, :] * np.asarray(exponents)[:, None] > -80.0
        )

    scan = np.concatenate(
        [
            power([1, steps, 2 * steps, 4 * steps]),
            (2 * root / (1 - root * root))[None],
            (1 / root)[None],
            power([strip]),
        ]
    )
    inner = power(np.arange(1, steps + 1))
    segs = power(steps * np.arange(SEG))
    strips = power(strip * np.arange(devices + 1))
    closing = 1.0 / (1.0 - power([2 * grid]))
    as32 = lambda x: x.astype(np.float32)
    return as32(scan), as32(inner), as32(segs), as32(segs[::-1]), as32(strips), as32(closing)


def clip(value, top):
    return jnp.minimum(jnp.maximum(value, 0), top)


def window_copies(tab, field, raw, sems):
    caps, wide = raw.shape[0], raw.shape[3]
    frame = wide - LANES
    angles, grid = field.shape[0], field.shape[3]
    copies = []
    for slot in range(caps):
        column = clip(tab(slot, 1), grid - frame)
        angle = clip(tab(slot, 2), angles - 1)
        block = jnp.minimum(column // LANES, (grid - wide) // LANES)
        start = pl.multiple_of(block * LANES, LANES)
        copy = pltpu.make_async_copy(
            field.at[angle, :, :, pl.ds(start, wide)], raw.at[slot], sems.at[slot]
        )
        copy.start()
        copies.append((copy, lax.rem(wide - (column - block * LANES), wide)))
    return copies


def window_values(copies, raw, slot, part):
    wide = raw.shape[3]
    return pltpu.roll(raw[slot, part], copies[slot][1], axis=1)[:, : wide - LANES].astype(bf16)


def decoded(package, ints):
    rows = package.shape[0]
    digits = package[rows - CODE_ROWS :, :LANES].astype(f32)
    ints[...] = (digits[0:1] * DIGIT + digits[1:2]).astype(jnp.int32)
    return lambda slot, i: ints[0, slot * FIELDS + i]


def plain(tab):
    return lambda slot, i: tab[slot, i]


def package_rows(caps, strip, frame, angles, grid):
    windows = caps * 2 * strip
    halo = angles * 2 * grid // frame
    return windows, halo


def pack_kernel(caps, tab, field, out, raw, last_rows, halo_buf, sems, row_sem):
    frame = out.shape[1]
    angles, _, strip, grid = field.shape
    at_halo, halo_rows = package_rows(caps, strip, frame, angles, grid)
    copies = window_copies(plain(tab), field, raw, sems)
    row_copy = pltpu.make_async_copy(
        field.at[:, :, pl.ds(strip - PAD, PAD), :], last_rows, row_sem.at[0]
    )
    row_copy.start()
    place = lax.broadcasted_iota(jnp.int32, (CODE_ROWS, frame), 1)
    row = lax.broadcasted_iota(jnp.int32, (CODE_ROWS, frame), 0)
    high = jnp.zeros((CODE_ROWS, frame), jnp.int32)
    low = jnp.zeros((CODE_ROWS, frame), jnp.int32)
    for slot in range(caps):
        for i in range(FIELDS):
            here = place == slot * FIELDS + i
            high = jnp.where(here, tab[slot, i] // DIGIT, high)
            low = jnp.where(here, lax.rem(tab[slot, i], DIGIT), low)
    code = jnp.where(row == 0, high, jnp.where(row == 1, low, 0))
    out[out.shape[0] - CODE_ROWS :] = code.astype(f32).astype(bf16)
    row_copy.wait()
    per_row = grid // frame
    for a in range(angles):
        for part in range(2):
            for k in range(per_row):
                i = (a * 2 + part) * per_row + k
                halo_buf[i : i + 1] = last_rows[a, part, PAD - 1 :, k * frame : (k + 1) * frame]
    left_over = halo_buf[...]
    for i in range(3):
        digit = left_over.astype(bf16)
        out[at_halo + i * halo_rows : at_halo + (i + 1) * halo_rows] = digit
        left_over = left_over - digit.astype(f32)
    for slot in range(caps):
        copies[slot][0].wait()
        for part in range(2):
            at = (slot * 2 + part) * strip
            out[at : at + strip] = window_values(copies, raw, slot, part)


def pack(tab, field, caps, frame):
    angles, _, strip, grid = field.shape
    at_halo, halo_rows = package_rows(caps, strip, frame, angles, grid)
    return pl.pallas_call(
        functools.partial(pack_kernel, caps),
        out_shape=jax.ShapeDtypeStruct((at_halo + 3 * halo_rows + CODE_ROWS, frame), bf16),
        in_specs=[SMEM_SPEC, ANY_SPEC],
        out_specs=VMEM_SPEC,
        scratch_shapes=[
            pltpu.VMEM((caps, 2, strip, frame + LANES), f32),
            pltpu.VMEM((angles, 2, PAD, grid), f32),
            pltpu.VMEM((halo_rows, frame), f32),
            pltpu.SemaphoreType.DMA((caps,)),
            pltpu.SemaphoreType.DMA((1,)),
        ],
        compiler_params=PARAMS,
        cost_estimate=cost(6),
        name="pack",
    )(tab, field)


def extract_kernel(coded, tab, field, *rest):
    raw, ints, sems = rest[-3:]
    out = rest[0] if coded else rest[1]
    read = decoded(tab, ints) if coded else plain(tab)
    copies = window_copies(read, field, raw, sems)
    for slot in range(out.shape[0]):
        copies[slot][0].wait()
        for part in range(2):
            out[slot, part] = window_values(copies, raw, slot, part)


def extract(tab, coded, field, caps, frame, package=None):
    angles, _, strip, grid = field.shape
    window = jax.ShapeDtypeStruct((caps, 2, strip, frame), bf16)
    through = [] if coded else [package]
    out = pl.pallas_call(
        functools.partial(extract_kernel, coded),
        out_shape=[window] + [jax.ShapeDtypeStruct(x.shape, x.dtype) for x in through],
        in_specs=[VMEM_SPEC if coded else SMEM_SPEC, ANY_SPEC] + [ANY_SPEC] * len(through),
        out_specs=[VMEM_SPEC] + [ANY_SPEC] * len(through),
        input_output_aliases={2: 1} if through else {},
        scratch_shapes=[
            pltpu.VMEM((caps, 2, strip, frame + LANES), f32),
            pltpu.VMEM((1, LANES), jnp.int32),
            pltpu.SemaphoreType.DMA((caps,)),
        ],
        compiler_params=PARAMS,
        cost_estimate=cost(2),
        name="extract",
    )(tab, field, *through)
    return out[0] if coded else out


def frame_kernel(reach, package, measured, probe, left, right, *rest):
    windows = rest[:reach]
    pieces = rest[reach : 2 * reach + 1]
    window_buf, update_buf, ints = rest[2 * reach + 1 :]
    caps, _, strip, frame = windows[0].shape
    read = decoded(package, ints)
    blocks = frame // LANES
    count = read(0, 3)
    probe_re, probe_im = probe[0], probe[1]
    peak = jnp.max(probe_re * probe_re + probe_im * probe_im) + epsilon_term
    for slot in range(caps):
        update_buf[...] = jnp.zeros_like(update_buf)

        @pl.when(slot < count)
        def _():
            offset = clip(read(slot, 0), strip - 1)
            for j in range(reach + 1):
                for part in range(2):
                    for k in range(blocks):
                        lanes = slice(k * LANES, (k + 1) * LANES)
                        at = (slot * 2 + part) * strip
                        values = (
                            windows[j - 1][slot, part, :, lanes]
                            if j
                            else package[at : at + strip, lanes]
                        )
                        window_buf[part, k, j * strip : (j + 1) * strip] = values.astype(f32)
            obj_re, obj_im = (
                jnp.concatenate(
                    [window_buf[part, k, pl.ds(offset, frame), :] for k in range(blocks)], axis=1
                )
                for part in range(2)
            )
            wave = jnp.concatenate(
                [
                    (probe_re * obj_re - probe_im * obj_im).astype(bf16),
                    (probe_re * obj_im + probe_im * obj_re).astype(bf16),
                ],
                axis=0,
            )

            def both(first, second, rows):
                first_half = jnp.dot(first, rows, preferred_element_type=f32).astype(bf16)
                beside = jnp.concatenate([first_half[:frame], first_half[frame:]], axis=1)
                return jnp.dot(beside, second, preferred_element_type=f32)

            spectrum = both(left[...], right[...], wave)
            spec_re, spec_im = spectrum[:, :frame], spectrum[:, frame:]
            power = spec_re * spec_re + spec_im * spec_im
            factor = (
                measured[slot].astype(f32)
                * lax.rsqrt(jnp.maximum(power, magnitude_floor**2)) - 1.0
            )
            change = jnp.concatenate(
                [(spec_re * factor).astype(bf16), (spec_im * factor).astype(bf16)], axis=0
            )
            correction = both(right[...], left[...], change)
            corr_re, corr_im = correction[:, :frame], correction[:, frame:]
            update = (
                (probe_re * corr_re + probe_im * corr_im) / peak,
                (probe_re * corr_im - probe_im * corr_re) / peak,
            )
            for part in range(2):
                for k in range(blocks):
                    update_buf[part, k, pl.ds(2 * PAD + offset, frame), :] = update[part][
                        :, k * LANES : (k + 1) * LANES
                    ]

        for part in range(2):
            for k in range(blocks):
                lanes = slice(k * LANES, (k + 1) * LANES)
                for j in range(reach + 1):
                    rim = PAD if j else 0
                    first = j * strip + 2 * PAD
                    pieces[j][slot, part, :, lanes] = update_buf[
                        part, k, first - rim : first + strip + rim
                    ].astype(pieces[j].dtype)


def run_frames(package, measured, probe, windows, center):
    reach = len(windows)
    caps, _, strip, frame = windows[0].shape
    left, right = fourier_blocks(frame)
    rows = (reach + 1) * strip
    piece = lambda j: jax.ShapeDtypeStruct(
        (caps, 2, strip + (2 * PAD if j else 0), frame), f32 if j == center else bf16
    )
    return pl.pallas_call(
        functools.partial(frame_kernel, reach),
        out_shape=[piece(j) for j in range(reach + 1)],
        in_specs=[VMEM_SPEC] * (5 + reach),
        out_specs=[VMEM_SPEC] * (reach + 1),
        scratch_shapes=[
            pltpu.VMEM((2, frame // LANES, rows, LANES), f32),
            pltpu.VMEM((2, frame // LANES, rows + 4 * PAD, LANES), f32),
            pltpu.VMEM((1, LANES), jnp.int32),
        ],
        compiler_params=PARAMS,
        cost_estimate=cost(5),
        name="frames",
    )(package, measured, probe, jnp.asarray(left), jnp.asarray(right), *windows)


def reversed_lanes(values):
    index = LANES - 1 - lax.broadcasted_iota(jnp.int32, values.shape, 1)
    return jnp.take_along_axis(values, index, axis=1)


def split_pair(values):
    high = values.astype(bf16)
    return high, (values - high.astype(f32)).astype(bf16)


def three_pass(rows, count, high, low):
    both = jnp.dot(rows, high, preferred_element_type=f32)
    return both[:count] + both[count:] + jnp.dot(rows[:count], low, preferred_element_type=f32)


def update_kernel(reach, center, *refs):
    tabs = refs[:reach]
    field, package, halo, scan, segs, table, *rest = refs[reach:]
    tabs = tabs[:center] + (None,) + tabs[center:]
    pieces = rest[: reach + 1]
    updated, inner, carry_y, carry_z, ends = rest[reach + 1 : reach + 6]
    ext, col_bond, source, edge, rows_in, ints, load_sems, store_sems = rest[reach + 6 :]
    angles, _, strip, grid = field.shape
    blocks = grid // LANES
    half_blocks = blocks // 2
    half = grid // 2
    steps = strip // SEG
    count = angles * strip + 2 * PAD
    caps = pieces[0].shape[0]
    frame = pieces[0].shape[3]
    frame_blocks = frame // LANES

    def load(a, b):
        start = b * LANES
        return pltpu.make_async_copy(
            field.at[a, :, :, pl.ds(start, LANES)],
            ext.at[a, :, b, pl.ds(PAD, strip), :],
            load_sems.at[a, b],
        )

    def store(a, b):
        start = b * LANES
        return pltpu.make_async_copy(
            ext.at[a, :, b, pl.ds(PAD, strip), :],
            updated.at[a, :, :, pl.ds(start, LANES)],
            store_sems.at[a, b],
        )

    for a in range(angles):
        for b in range(blocks):
            load(a, b).start()
    halo_rows = halo.shape[0] // 3
    top = sum(halo[i * halo_rows : (i + 1) * halo_rows].astype(f32) for i in range(3))
    per_row = grid // frame
    read = decoded(package, ints)
    for a in range(angles):
        for part in range(2):
            for b in range(blocks):
                row = (a * 2 + part) * per_row + b // frame_blocks
                lanes = slice(b % frame_blocks * LANES, (b % frame_blocks + 1) * LANES)
                ext[a, part, b, PAD - 1 : PAD, :] = top[row : row + 1, lanes]
            ext[a, part, blocks] = jnp.zeros((strip + 2 * PAD, LANES), f32)
    for a in range(angles):
        for b in range(blocks):
            load(a, b).wait()

    def add_piece(piece, tab, slot):
        @pl.when(slot < tab(0, 3))
        def _():
            column = clip(tab(slot, 1), grid - frame)
            angle = clip(tab(slot, 2), angles - 1)
            block = jnp.minimum(column // LANES, blocks - frame_blocks - 1)
            shift = column - block * LANES
            for part in range(2):
                values = piece[slot, part].astype(f32)
                rows = values.shape[0]
                first = PAD + (strip - rows) // 2
                values = jnp.concatenate([values, jnp.zeros((rows, LANES), f32)], axis=1)
                values = pltpu.roll(values, shift, axis=1)
                for k in range(frame_blocks + 1):
                    spot = ext.at[angle, part, block + k, first : first + rows]
                    spot[...] += values[:, k * LANES : (k + 1) * LANES]

    for slot in range(caps):
        for j in range(reach + 1):
            add_piece(pieces[j], read if j == center else plain(tabs[j]), slot)

    for a in range(angles):
        for b in range(blocks):
            store(a, b).start()

    lane = lax.broadcasted_iota(jnp.int32, (SEG, LANES), 1)
    sub = lax.broadcasted_iota(jnp.int32, (SEG, LANES), 0)

    def power_of(re, im):
        return re * re + (im * im + 0.5 * soften_term)

    def bond(re, im, power, re_to, im_to):
        return (re * im_to - im * re_to) * pl.reciprocal(
            power + power_of(re_to, im_to), approx=True
        )

    for a in range(angles):
        col_bond[...] = jnp.zeros_like(col_bond)

        def columns(b, _, a=a):
            def cells(first, block):
                return ext[a, 0, block, first : first + SEG], ext[a, 1, block, first : first + SEG]

            groups = strip // SEG
            re, im = cells(0, b)
            above = bond(re, im, power_of(re, im), *cells(1, b))
            edge[a, b] = -above[SEG - 1 :]
            batch = min(BATCH, groups)
            for g0 in range(0, groups, batch):
                firsts = [PAD + (g0 + i) * SEG for i in range(batch)]
                here = [cells(first, b) for first in firsts]
                to_right = [
                    [
                        pltpu.roll(jnp.where(lane == 0, after, now), LANES - 1, axis=1)
                        for now, after in zip(here[i], cells(firsts[i], b + 1))
                    ]
                    for i in range(batch)
                ]
                powers = [power_of(*here[i]) for i in range(batch)]
                downs = [bond(*here[i], powers[i], *cells(firsts[i] + 1, b)) for i in range(batch)]
                if g0 + batch == groups:
                    downs[-1] = jnp.where(sub == SEG - 1, 0.0, downs[-1])
                rights = [bond(*here[i], powers[i], *to_right[i]) for i in range(batch)]
                rows = [slice((g0 + i) * SEG, (g0 + i + 1) * SEG) for i in range(batch)]
                from_left = [
                    pltpu.roll(
                        jnp.where(lane == LANES - 1, col_bond[rows[i]], rights[i]), 1, axis=1
                    )
                    for i in range(batch)
                ]
                values = []
                for i in range(batch):
                    from_above = pltpu.roll(
                        jnp.where(sub == SEG - 1, above, downs[i]), 1, axis=0
                    )
                    above = downs[i]
                    values.append(from_above - downs[i] + from_left[i] - rights[i])
                for i in range(batch):
                    col_bond[rows[i]] = rights[i]
                    source[a, b, rows[i]] = values[i]
            return 0

        lax.fori_loop(0, blocks, columns, 0, unroll=4)

    def fold(b, _):
        lanes = pl.ds(pl.multiple_of(b * LANES, LANES), LANES)
        for a in range(angles):
            for t in range(0, steps, 2):
                lower = jnp.concatenate(
                    [source[a, b, pl.ds(t + i, SEG, stride=steps), :] for i in range(2)], 0
                )
                upper = jnp.concatenate(
                    [
                        source[a, blocks - 1 - b, pl.ds(t + i, SEG, stride=steps), :]
                        for i in range(2)
                    ],
                    0,
                )
                upper = reversed_lanes(upper)
                at = a * strip + t * SEG
                for h, values in enumerate((lower + upper, lower - upper)):
                    high, low = split_pair(values)
                    rows_in[h, at : at + 2 * SEG, lanes] = high
                    rows_in[h, count + at : count + at + 2 * SEG, lanes] = low
        edges = [jnp.concatenate([edge[a, i] for a in range(angles)], 0) for i in (b, blocks - 1 - b)]
        fill = jnp.zeros((2 * PAD - angles, LANES), f32)
        lower, upper = (jnp.concatenate([rows, fill], 0) for rows in edges)
        upper = reversed_lanes(upper)
        at = angles * strip
        for h, values in enumerate((lower + upper, lower - upper)):
            high, low = split_pair(values)
            rows_in[h, at : at + 2 * PAD, lanes] = high
            rows_in[h, count + at : count + at + 2 * PAD, lanes] = low
        return 0

    lax.fori_loop(0, half_blocks, fold, 0, unroll=4)

    wide = min(2 * LANES, half)
    sub = lax.broadcasted_iota(jnp.int32, (SEG, wide), 0)
    for h in range(2):

        def transform(c, _, h=h):
            lanes = pl.ds(pl.multiple_of(c * wide, wide), wide)
            spots = pl.ds(pl.multiple_of(h * half + c * wide, wide), wide)
            values = three_pass(rows_in[h], count, table[0, h, :, lanes], table[1, h, :, lanes])
            root = jnp.broadcast_to(scan[0:1, spots], (SEG, wide))
            for a in range(angles):
                terms = [
                    values[a * strip + t * SEG : a * strip + (t + 1) * SEG] for t in range(steps)
                ]
                down = [terms[0]]
                for t in range(1, steps):
                    down.append(terms[t] + root * down[-1])
                up = terms[steps - 1]
                inner[a, (steps - 1) * SEG : steps * SEG, spots] = down[steps - 1]
                for t in range(steps - 2, -1, -1):
                    after = root * up
                    inner[a, t * SEG : (t + 1) * SEG, spots] = down[t] + after
                    up = terms[t] + after
                tail_y, tail_z = down[steps - 1], up
                for i, k in enumerate((1, 2, 4)):
                    factor = scan[i + 1 : i + 2, spots]
                    tail_y = tail_y + jnp.where(
                        sub >= k, factor * pltpu.roll(tail_y, k, axis=0), 0.0
                    )
                    tail_z = tail_z + jnp.where(
                        sub < SEG - k, factor * pltpu.roll(tail_z, SEG - k, axis=0), 0.0
                    )
                above = values[angles * strip + a : angles * strip + a + 1]
                carry_y[a, :, spots] = (
                    jnp.where(sub >= 1, pltpu.roll(tail_y, 1, axis=0), 0.0) + segs[:, spots] * above
                )
                carry_z[a, :, spots] = jnp.where(
                    sub < SEG - 1, pltpu.roll(tail_z, SEG - 1, axis=0), 0.0
                )
                ends[0, a : a + 1, spots] = tail_z[0:1] + scan[5:6, spots] * above
                ends[1, a : a + 1, spots] = tail_y[SEG - 1 : SEG] + scan[6:7, spots] * above
            return 0

        lax.fori_loop(0, half // wide, transform, 0, unroll=4)

    for a in range(angles):
        for b in range(blocks):
            store(a, b).wait()


def run_update(tabs, field, package, halo, scan, segs, tables, pieces, center):
    angles, _, strip, grid = field.shape
    reach = len(pieces) - 1
    blocks = grid // LANES
    half = grid // 2
    return pl.pallas_call(
        functools.partial(update_kernel, reach, center),
        out_shape=[
            jax.ShapeDtypeStruct(field.shape, f32),
            jax.ShapeDtypeStruct((angles, strip, grid), f32),
            jax.ShapeDtypeStruct((angles, SEG, grid), f32),
            jax.ShapeDtypeStruct((angles, SEG, grid), f32),
            jax.ShapeDtypeStruct((2, angles, grid), f32),
        ],
        in_specs=[SMEM_SPEC] * reach
        + [ANY_SPEC]
        + [VMEM_SPEC] * (reach + 6),
        out_specs=[ANY_SPEC] + [VMEM_SPEC] * 4,
        scratch_shapes=[
            pltpu.VMEM((angles, 2, blocks + 1, strip + 2 * PAD, LANES), f32),
            pltpu.VMEM((strip, LANES), f32),
            pltpu.VMEM((angles, blocks, strip, LANES), f32),
            pltpu.VMEM((angles, blocks, 1, LANES), f32),
            pltpu.VMEM((2, 2 * (angles * strip + 2 * PAD), half), bf16),
            pltpu.VMEM((1, LANES), jnp.int32),
            pltpu.SemaphoreType.DMA((angles, blocks)),
            pltpu.SemaphoreType.DMA((angles, blocks)),
        ],
        compiler_params=UPDATE_PARAMS,
        cost_estimate=cost(14),
        name="update",
    )(*tabs, field, package, halo, scan, segs, tables, *pieces)


def phase_kernel(inner, carry_y, carry_z, enter, scan, powers, segs, segs_back, tables, out_hbm, rest, rows_in, table, out, table_sems, out_sems):
    angles, strip, grid = inner.shape
    half = grid // 2
    steps = strip // SEG
    count = angles * strip
    half_blocks = half // LANES
    wide = min(2 * LANES, half)
    chunks = half // wide

    def load_table(c):
        lanes = pl.ds(pl.multiple_of(c * wide, wide), wide)
        return pltpu.make_async_copy(
            tables.at[1, :, :, :, lanes], table.at[:, :, :, lanes], table_sems.at[c]
        )

    def store(c, side):
        start = c * wide if side == 0 else grid - (c + 1) * wide
        lanes = pl.ds(pl.multiple_of(start, wide), wide)
        return pltpu.make_async_copy(
            out.at[:, :, lanes], out_hbm.at[:, :, lanes], out_sems.at[c, side]
        )

    for c in range(chunks):
        load_table(c).start()

    def solve(b, _):
        spots = pl.ds(pl.multiple_of(b * LANES, LANES), LANES)
        scale = scan[4:5, spots]
        for a in range(angles):
            from_y = scale * (carry_y[a, :, spots] + segs[:, spots] * enter[0, a : a + 1, spots])
            from_z = scale * (carry_z[a, :, spots] + segs_back[:, spots] * enter[1, a : a + 1, spots])
            for t in range(steps):
                rest[a, b, pl.ds(t, SEG, stride=steps), :] = (
                    scale * inner[a, t * SEG : (t + 1) * SEG, spots]
                    + powers[t : t + 1, spots] * from_y
                    + powers[steps - 1 - t : steps - t, spots] * from_z
                )
        return 0

    lax.fori_loop(0, 2 * half_blocks, solve, 0, unroll=4)

    def split(b, _):
        lanes = pl.ds(pl.multiple_of(b * LANES, LANES), LANES)
        for h in range(2):
            for a in range(angles):
                high, low = split_pair(rest[a, h * half_blocks + b])
                rows_in[h, a * strip : (a + 1) * strip, lanes] = high
                rows_in[h, count + a * strip : count + (a + 1) * strip, lanes] = low
        return 0

    lax.fori_loop(0, half_blocks, split, 0, unroll=2)

    def back(c, _):
        lanes = pl.ds(pl.multiple_of(c * wide, wide), wide)
        load_table(c).wait()
        even, odd = (
            three_pass(rows_in[h], count, table[0, h, :, lanes], table[1, h, :, lanes])
            for h in range(2)
        )
        mirrored = even - odd
        plain = even + odd
        for a in range(angles):
            out[a, :, lanes] = plain[a * strip : (a + 1) * strip]
            for k in range(wide // LANES):
                spot = pl.ds(
                    pl.multiple_of(grid - (k + 1) * LANES - c * wide, LANES), LANES
                )
                out[a, :, spot] = reversed_lanes(
                    mirrored[a * strip : (a + 1) * strip, k * LANES : (k + 1) * LANES]
                )
        for side in range(2):
            store(c, side).start()
        return 0

    lax.fori_loop(0, chunks, back, 0, unroll=4)
    for c in range(chunks):
        for side in range(2):
            store(c, side).wait()


def run_phase(inner, carry_y, carry_z, enter, scan, powers, segs, segs_back, tables):
    angles, strip, grid = inner.shape
    half = grid // 2
    chunks = half // min(2 * LANES, half)
    return pl.pallas_call(
        phase_kernel,
        out_shape=jax.ShapeDtypeStruct((angles, strip, grid), f32),
        in_specs=[VMEM_SPEC] * 8 + [ANY_SPEC],
        out_specs=ANY_SPEC,
        scratch_shapes=[
            pltpu.VMEM((angles, grid // LANES, strip, LANES), f32),
            pltpu.VMEM((2, 2 * angles * strip, half), bf16),
            pltpu.VMEM(tables.shape[1:], bf16),
            pltpu.VMEM((angles, strip, grid), f32),
            pltpu.SemaphoreType.DMA((chunks,)),
            pltpu.SemaphoreType.DMA((chunks, 2)),
        ],
        compiler_params=PHASE_PARAMS,
        cost_estimate=cost(7),
        name="phase",
    )(inner, carry_y, carry_z, enter, scan, powers, segs, segs_back, tables)


def passed_along(x, by):
    size = lax.axis_size("tile")
    pairs = [(i, i + by) for i in range(size) if 0 <= i + by < size]
    return lax.ppermute(x, "tile", pairs)


def entering_values(ends, strips, closing):
    size = lax.axis_size("tile")
    me = lax.axis_index("tile")
    head, tail = ends[0], ends[1]
    enter_y = jnp.zeros_like(head)
    enter_z = jnp.zeros_like(head)
    row = lambda i: lax.dynamic_slice_in_dim(strips, i, 1, 0)
    width = 1
    while width < size:
        other = lax.ppermute(
            jnp.stack([head, tail]), "tile", [(i, i ^ width) for i in range(size)]
        )
        head_to, tail_to = other[0], other[1]
        second = (me & width) != 0
        before = me & (width - 1)
        span = strips[width : width + 1]
        enter_y = enter_y + jnp.where(second, row(before) * tail_to, 0.0)
        enter_z = enter_z + jnp.where(second, 0.0, row(width - 1 - before) * head_to)
        head, tail = (
            jnp.where(second, head_to + span * head, head + span * head_to),
            jnp.where(second, tail + span * tail_to, tail_to + span * tail),
        )
        width *= 2
    whole = strips[size : size + 1]
    enter_y = enter_y + row(me) * (head + whole * tail) * closing
    enter_z = enter_z + row(size - 1 - me) * (tail + whole * head) * closing
    return jnp.stack([enter_y, enter_z])


def body(object_field, probe, measured, frame_table, frame_count):
    angles, _, strip, grid = object_field.shape
    caps, frame = measured.shape[0], measured.shape[1]
    reach = frame // strip
    center = reach // 2
    halves = cosine_halves(grid)
    forward = jnp.asarray(split_table(np.swapaxes(halves, 1, 2)))
    tables = jnp.asarray(np.stack([split_table(np.swapaxes(halves, 1, 2)), split_table(halves)]))
    scan, powers, segs, segs_back, strips, closing = (
        jnp.asarray(x) for x in decay_tables(grid, strip)
    )

    own_tab = jnp.concatenate(
        [frame_table, jnp.broadcast_to(frame_count[None, :], (caps, 1))], axis=1
    )
    far = [j for j in range(1, reach + 1) if j != center]
    tabs = {0: own_tab}
    for j in far:
        tabs[j] = passed_along(own_tab, j)
    measured_here = passed_along(measured, center)
    package = pack(own_tab, object_field, caps, frame)
    windows = {}
    for j in far:
        window, package = extract(tabs[j], False, object_field, caps, frame, package)
        windows[j] = passed_along(window, center - j)
    arrived = passed_along(package, center)
    at_halo, halo_rows = package_rows(caps, strip, frame, angles, grid)
    halo = slice(at_halo, at_halo + 3 * halo_rows)
    top = arrived[halo] if center == 1 else passed_along(package[halo], 1)
    windows[center] = extract(arrived, True, object_field, caps, frame)
    pieces = run_frames(arrived, measured_here, probe, [windows[j] for j in range(1, reach + 1)], center)
    pieces = [
        piece if j == center else passed_along(piece, j - center) for j, piece in enumerate(pieces)
    ]
    updated, inner, carry_y, carry_z, ends = run_update(
        [tabs[j] for j in range(reach + 1) if j != center],
        object_field,
        arrived,
        top,
        scan,
        segs,
        forward,
        pieces,
        center,
    )
    enter = entering_values(ends, strips, closing)
    phase_map = run_phase(
        inner, carry_y, carry_z, enter, scan, powers, segs, segs_back, tables
    )
    return (updated, phase_map)


def solution(mesh):
    return jax.shard_map(
        body,
        mesh=mesh,
        in_specs=(
            P("group", None, "tile", None),
            P(),
            P(("group", "tile"), None, None),
            P(("group", "tile"), None),
            P(("group", "tile")),
        ),
        out_specs=(P("group", None, "tile", None), P("group", "tile", None)),
        check_vma=False,
    )
```
